32 devices in a mesh: seq: 4 (over y, x), shard: 8 (over z, core).
Axes of the slice: x: 2, y: 2, z: 4, core: 2. Of those that a mesh axis runs over, the one named last changes fastest.
Arguments:
- tokens: bfloat16 [8, 4096, 768], P('shard', 'seq'), may hold values from -6 to 6
- cotangent: bfloat16 [8, 4096, 768], P('shard', 'seq'), may hold values from -6 to 6
- seg_ids: int32 [8, 4096], P('shard'), may hold values from 0 to 2, as said below
- norm_gain: bfloat16 [2, 768], P(None, 'shard'), may hold values from 0.5 to 1.5
- in_weight: bfloat16 [2, 768, 3328], P(None, 'shard'), may hold values from -0.21875 to 0.21875
- dt_weight: bfloat16 [2, 768, 24], P(None, 'shard'), may hold values from -0.21875 to 0.21875
- conv_weight: bfloat16 [2, 4, 1792], P(None, None, 'shard'), may hold values from -3 to 3
- conv_bias: bfloat16 [2, 1792], P(None, 'shard'), may hold values from -1.5 to 1.5
- dt_bias: float32 [2, 24], P(None, 'seq'), may hold values from -6.5 to -2.3
- a_log: float32 [2, 24], P(None, 'seq'), may hold values from 0 to 2.77
- skip: float32 [2, 24], P(None, 'seq'), may hold values from 0.5 to 1.5
- out_gain: bfloat16 [2, 1536], P(None, 'shard'), may hold values from 0.5 to 1.5
- out_weight: bfloat16 [2, 1536, 768], P(None, 'shard'), may hold values from -0.15625 to 0.15625
Outputs:
- activations: bfloat16 [8, 4096, 768], P('shard', 'seq')
- input_grad: float32 [8, 4096, 768], P('shard', 'seq')
- grad_norm_gain: float32 [2, 768], P(None, 'shard')
- grad_in_weight: float32 [2, 768, 3328], P(None, 'shard')
- grad_dt_weight: float32 [2, 768, 24], P(None, 'shard')
- grad_conv_weight: float32 [2, 4, 1792], P(None, None, 'shard')
- grad_conv_bias: float32 [2, 1792], P(None, 'shard')
- grad_dt_bias: float32 [2, 24], P(None, 'seq')
- grad_a_log: float32 [2, 24], P(None, 'seq')
- grad_skip: float32 [2, 24], P(None, 'seq')
- grad_out_gain: float32 [2, 1536], P(None, 'shard')
- grad_out_weight: float32 [2, 1536, 768], P(None, 'shard')
The draws below stay inside these ranges and needn't reach their ends.
Inputs may be any that keep to these rules, and one draw needn't show every extreme that they name: `seg_ids`: in each stream the ids never fall; id 1 begins within the first 1024 tokens and ends within the last 1024.
All inputs are finite; a program needn't handle non-finite values.
Results may differ from the reference program's by a relative error of at most 0.02.
Values may be sent and summed in bfloat16 or wider, within the bound.
No kernel may reach another device: no remote copies, remote signals or barrier semaphores. Data moves between devices by JAX's collectives and lax.ppermute only.
A program may use at most 320 MiB of HBM per device.

```python
import jax
import jax.numpy as jnp
from jax import lax

D = 768
HEADS = 24
CONV = 4
SPAN = 256
LAYERS = 2
TOK_DEV = 1024
INNER = 1536
CHANNELS = 1792
PROJ = 3328
STREAM = 4096
STREAMS = 8


def draw_seg_ids(key, part):
    key = jax.random.fold_in(key, 11)
    first_key, last_key = jax.random.split(key)
    first = jax.random.randint(first_key, (STREAMS, 1), 1, TOK_DEV)
    last = jax.random.randint(last_key, (STREAMS, 1), STREAM - TOK_DEV + 1, STREAM)
    where = jnp.arange(STREAM, dtype=jnp.int32)[None, :]
    return (where >= first).astype(jnp.int32) + (where >= last).astype(jnp.int32)


def block_levels(key, shape, shards, low, largest):
    def one(axis_at, shards_of):
        draws = jax.random.uniform(jax.random.fold_in(jax.random.fold_in(key, 6), axis_at), (shards_of,), jnp.float32, low / len(shards), largest / len(shards))
        return jnp.repeat(jnp.exp(draws), shape[axis_at] // shards_of).reshape((-1,) + (1,) * (len(shape) - axis_at - 1))

    level = one(*shards[0])
    for cut in shards[1:]:
        level = level * one(*cut)
    return level


def centred(stream_key, dims, deviation, most, pieces=(), held_as=jnp.bfloat16):
    factor_of = block_levels(stream_key, dims, pieces, -0.22, 0.18) if pieces else 1.0
    entries = jax.random.normal(stream_key, dims, jnp.float32) * deviation * factor_of
    return jnp.minimum(jnp.maximum(entries, -most), most).astype(held_as)


def setup_inputs(seed: int = 0) -> dict:
    seeds = jax.random.split(jax.random.key(seed), 14)
    return {
        "tokens": centred(seeds[0], (STREAMS, STREAM, D), 1.0, 6.0, ((0, 8), (1, 4))),
        "cotangent": centred(seeds[1], (STREAMS, STREAM, D), 1.0, 6.0, ((0, 8), (1, 4))),
        "seg_ids": draw_seg_ids(jax.random.fold_in(seeds[13], 71), 0),
        "norm_gain": jnp.clip(1.0 + 0.1 * jax.random.normal(seeds[3], (LAYERS, D), jnp.float32), 0.5, 1.5).astype(jnp.bfloat16),
        "in_weight": centred(seeds[4], (LAYERS, D, PROJ), D ** -0.5, 0.21875, ((1, 8),)),
        "dt_weight": centred(seeds[5], (LAYERS, D, HEADS), D ** -0.5, 0.21875, ((1, 8),)),
        "conv_weight": centred(seeds[6], (LAYERS, CONV, CHANNELS), CONV ** -0.5, 3.0, ((2, 8),)),
        "conv_bias": centred(seeds[7], (LAYERS, CHANNELS), 0.3, 1.5, ((1, 8),)),
        "dt_bias": jnp.clip(-6.5 + 4.2 * jax.random.uniform(seeds[8], (LAYERS, HEADS), jnp.float32) ** block_levels(seeds[8], (LAYERS, HEADS), ((1, 4),), -0.2, 0.2), -6.5, -2.3),
        "a_log": jnp.clip(2.77 * jax.random.uniform(seeds[9], (LAYERS, HEADS), jnp.float32) ** block_levels(seeds[9], (LAYERS, HEADS), ((1, 4),), -0.2, 0.2), 0.0, 2.77),
        "skip": jnp.clip(0.5 + 1.0 * jax.random.uniform(seeds[10], (LAYERS, HEADS), jnp.float32) ** block_levels(seeds[10], (LAYERS, HEADS), ((1, 4),), -0.2, 0.2), 0.5, 1.5),
        "out_gain": jnp.clip(1.0 + 0.1 * jax.random.normal(seeds[11], (LAYERS, INNER), jnp.float32), 0.5, 1.5).astype(jnp.bfloat16),
        "out_weight": centred(seeds[12], (LAYERS, INNER, D), INNER ** -0.5, 0.15625, ((1, 8),)),
    }


@jax.custom_vjp
def low(v):
    return lax.optimization_barrier(v.astype(jnp.bfloat16)).astype(jnp.float32)

@jax.custom_vjp
def low_back(v):
    return v

def low_keep(v):
    return (low(v), None)

def low_pass(kept, grad):
    return (grad,)

def back_keep(v):
    return (v, None)

def back_low(kept, grad):
    return (low(grad),)
low.defvjp(low_keep, low_pass)
low_back.defvjp(back_keep, back_low)
EPS = 1e-05
HIGH = lax.Precision.HIGHEST

def matmul(left, right):
    return jnp.dot(left, right, precision=HIGH)

def rms(value, gain):
    return value * lax.rsqrt(lax.optimization_barrier(jnp.mean(value * value, axis=-1, keepdims=True)) + EPS) * gain

def convolve(xbc, weight, bias, ids):
    taps = weight.shape[0]
    count = xbc.shape[0]
    padded = jnp.concatenate([jnp.zeros((taps - 1, xbc.shape[1]), xbc.dtype), xbc])
    padded_ids = jnp.concatenate([jnp.full((taps - 1,), -1, jnp.int32), ids.astype(jnp.int32)])
    total = bias + jnp.zeros_like(xbc)
    for tap in range(taps):
        valid = (padded_ids[tap:tap + count] == ids)[:, None].astype(xbc.dtype)
        total = total + weight[tap] * padded[tap:tap + count] * valid
    return total

def mixing(x, dt_raw, bc, dt_bias, a_log, skip, ids):
    length, heads = dt_raw.shape
    width = x.shape[1] // heads
    state = bc.shape[1] // 2
    blocks = length // SPAN
    step = jax.nn.softplus(dt_raw + dt_bias)
    rate = step * -jnp.exp(a_log)
    xs = x.reshape(blocks, SPAN, heads, width)
    steps = step.reshape(blocks, SPAN, heads)
    inb = bc[:, :state].reshape(blocks, SPAN, state)
    outb = bc[:, state:].reshape(blocks, SPAN, state)
    tags = ids.astype(jnp.int32).reshape(blocks, SPAN)
    cumul = jnp.cumsum(rate.reshape(blocks, SPAN, heads), axis=1)
    lower = jnp.arange(SPAN)[:, None] >= jnp.arange(SPAN)[None, :]
    same = ((tags[:, :, None] == tags[:, None, :]) & lower)[..., None]
    gap = cumul[:, :, None, :] - cumul[:, None, :, :]
    decay = jnp.where(same, jnp.exp(jnp.where(same, gap, 0.0)), 0.0)
    scores = jnp.einsum('bqn,bsn->bqs', outb, inb, precision=HIGH)
    driven = steps[..., None] * xs
    inside = jnp.einsum('bqs,bqsh,bshp->bqhp', scores, decay, driven, precision=HIGH)
    last = tags[:, -1:]
    toend = jnp.where((tags == last)[..., None], jnp.exp(cumul[:, -1:, :] - cumul), 0.0)
    local = jnp.einsum('bsh,bshp,bsn->bhpn', toend, driven, inb, precision=HIGH)
    before = jnp.concatenate([jnp.full((1,), -1, jnp.int32), tags[:-1, -1]])
    factor = jnp.where((tags[:, -1] == before)[:, None], jnp.exp(cumul[:, -1, :]), 0.0)

    def advance(carry, item):
        scale, fresh = item
        return (scale[:, None, None] * carry + fresh, carry)
    start = jnp.zeros((heads, width, state), x.dtype)
    _, entering = lax.scan(advance, start, (factor, local))
    reach = jnp.where((tags == before[:, None])[..., None], jnp.exp(cumul), 0.0)
    across = reach[..., None] * jnp.einsum('bqn,bhpn->bqhp', outb, entering, precision=HIGH)
    result = inside + across + skip[:, None] * xs
    return result.reshape(length, heads * width)

def stack(hidden, weights, ids):
    gains_in, w_in, w_dt, w_conv, b_conv, dt_bias, a_log, skip, gains_out, w_out = weights
    for layer in range(LAYERS):
        normed = low(rms(hidden, gains_in[layer]))
        project = low_back(matmul(normed, w_in[layer]))
        dt_raw = low(low_back(matmul(normed, w_dt[layer])))
        gate_z = project[:, :INNER]
        conv_in = low(project[:, INNER:])
        active = low(low_back(jax.nn.silu(convolve(conv_in, w_conv[layer], b_conv[layer], ids))))
        mixed = jax.checkpoint(mixing)(active[:, :INNER], dt_raw, active[:, INNER:], dt_bias[layer], a_log[layer], skip[layer], ids)
        mixed = low(low_back(mixed))
        gated = low(rms(mixed * jax.nn.silu(gate_z), gains_out[layer]))
        hidden = hidden + low_back(matmul(gated, w_out[layer]))
    return hidden

def reference(tokens, cotangent, seg_ids, norm_gain, in_weight, dt_weight, conv_weight, conv_bias, dt_bias, a_log, skip, out_gain, out_weight):
    params = tuple((p.astype(jnp.float32) for p in (norm_gain, in_weight, dt_weight, conv_weight, conv_bias, dt_bias, a_log, skip, out_gain, out_weight)))

    def stream_step(total, item):
        start, cot, ids = item

        def forward(hidden, weights):
            return stack(hidden, weights, ids)
        out, pull = jax.vjp(forward, start.astype(jnp.float32), params)
        d_start, d_weights = pull(cot.astype(jnp.float32))
        total = jax.tree.map(lambda a, b: a + b, total, d_weights)
        return (total, (out.astype(jnp.bfloat16), d_start))
    zeros = jax.tree.map(jnp.zeros_like, params)
    total, (acts, d_in) = lax.scan(stream_step, zeros, (tokens, cotangent, seg_ids))
    return (acts, d_in, total[0], total[1], total[2], total[3], total[4], total[5], total[6], total[7], total[8], total[9])
```

```python
import functools

import jax
import jax.numpy as jnp
from jax import lax
from jax.experimental import pallas as pl
from jax.experimental.pallas import tpu as pltpu
from jax.sharding import PartitionSpec as P

CONV = 4
EPS = 1e-05
CHUNK = 128
EDGE = 16
LOG2E = 1.4426950408889634
FAR = -1e30
BF = jnp.bfloat16
F32 = jnp.float32
HIGH = lax.Precision.HIGHEST
VMEM = 56 * 1024 * 1024


def dot(left, right, left_dim, right_dim, precision=None):
    return lax.dot_general(
        left,
        right,
        (((left_dim,), (right_dim,)), ((), ())),
        precision=precision,
        preferred_element_type=F32,
    )


def col_sum(value):
    return jnp.sum(value, axis=0, keepdims=True)


def sigmoid(value):
    return 0.5 * jnp.tanh(0.5 * value) + 0.5


def per_head(rows, first, count, width):
    return jnp.concatenate(
        [jnp.broadcast_to(rows[k : k + 1], (width, rows.shape[1])) for k in range(first, first + count)]
    )


def iotas():
    down = lax.broadcasted_iota(jnp.int32, (CHUNK, CHUNK), 0)
    across = lax.broadcasted_iota(jnp.int32, (CHUNK, CHUNK), 1)
    return down, across


def step_sizes(raw, bias, log_rate):
    shifted = raw + bias
    step = jnp.maximum(shifted, 0.0) + jnp.log1p(jnp.exp(-jnp.abs(shifted)))
    rate = -jnp.exp(log_rate)
    down, across = iotas()
    upto = (down <= across).astype(F32)
    running = dot(step * (rate * LOG2E), upto, 1, 0, HIGH)
    return shifted, step, rate, running


def pair_mask(info):
    down, across = iotas()
    tags = info[0:8]
    column = jnp.transpose(tags)[:, 0:1]
    reaches = (column == info[0:1]) & (down <= across)
    return jnp.where(reaches, 0.0, FAR)


def chunk_factors(running, info):
    total = running[:, CHUNK - 1 : CHUNK]
    reach = jnp.exp2(running) * info[7:8]
    toend = jnp.exp2(total - running) * info[8:9]
    whole = jnp.exp2(jnp.broadcast_to(total, running.shape)) * info[9:10]
    return reach, toend, whole


def shape_of(heads, inner, state):
    width = inner // heads
    return width, CHUNK // width, inner // CHUNK


def conv_block(cur, prev, taps, bias, info):
    lane = lax.broadcasted_iota(jnp.int32, cur.shape, 1)
    total = bias + taps[CONV - 1] * cur
    for k in range(1, CONV):
        mixed = jnp.where(lane >= CHUNK - k, prev, cur)
        total = total + taps[CONV - 1 - k] * (pltpu.roll(mixed, k, 1) * info[k : k + 1])
    return total


def scan_kernel(
    heads,
    inner,
    qd_ref,
    halo_ref,
    taps_ref,
    bias_ref,
    log_ref,
    skip_ref,
    info_ref,
    xa_ref,
    slope_ref,
    part_ref,
    enter_ref,
    prefix_ref,
    reach_ref,
    pack_ref,
    carry,
    wide,
    state,
    prefix,
):
    step_at = pl.program_id(0)
    last = pl.num_programs(0) - 1
    channels = xa_ref.shape[0]
    padded = bias_ref.shape[0]
    n_state = (channels - inner) // 2
    width, group, blocks = shape_of(heads, inner, n_state)

    @pl.when(step_at == 0)
    def _():
        for at in range(0, channels, CHUNK):
            rows = halo_ref[:, at : at + CHUNK].astype(F32)
            rows = jnp.concatenate([jnp.zeros((CHUNK - EDGE, CHUNK), F32), rows])
            carry[at : at + CHUNK, :] = jnp.transpose(rows).astype(BF)
            for k in range(CONV + 1):
                wide[k, at : at + CHUNK, :] = jnp.broadcast_to(
                    taps_ref[at : at + CHUNK, k : k + 1], (CHUNK, CHUNK)
                )
        state[...] = jnp.zeros_like(state)
        prefix[...] = jnp.ones_like(prefix)

    info = info_ref[...]
    raw = qd_ref[channels : channels + padded, :].astype(F32)
    _, step, _, running = step_sizes(raw, bias_ref[...], log_ref[...])
    reach, toend, whole = chunk_factors(running, info)
    before = prefix[...]
    prefix_ref[0] = before
    reach_ref[...] = before * reach
    prefix[...] = before * whole
    column = jnp.transpose(running)
    mask = pair_mask(info)
    skip = skip_ref[...]

    def active(at):
        rows = pl.ds(at, CHUNK)
        pre = conv_block(
            qd_ref[rows, :].astype(F32),
            carry[rows, :].astype(F32),
            [wide[k, rows, :] for k in range(CONV)],
            wide[CONV, rows, :],
            info,
        )
        gate = sigmoid(pre)
        value = (pre * gate).astype(BF)
        xa_ref[rows, :] = value
        slope_ref[rows, :] = (gate * (1.0 + pre * (1.0 - gate))).astype(BF)
        return value

    in_t = active(inner)
    out_t = active(inner + n_state)
    scores = dot(in_t, out_t, 0, 0)
    for block in range(blocks):
        at = block * CHUNK
        rows = pl.ds(at, CHUNK)
        x = active(at).astype(F32)
        first = block * group
        entering = state[rows, :]
        entering_low = entering.astype(BF)
        enter_ref[0, rows, :] = entering_low
        driven = x * per_head(step, first, group, width)
        total = x * per_head(skip, first, group, width) + per_head(
            reach, first, group, width
        ) * dot(entering_low, out_t, 1, 0)
        driven_low = driven.astype(BF)
        inside = []
        for k in range(group):
            head = first + k
            gap = (running[head : head + 1] + mask) - column[:, head : head + 1]
            mixer = (scores * jnp.exp2(gap)).astype(BF)
            inside.append(dot(driven_low[k * width : (k + 1) * width], mixer, 1, 0))
        part_ref[rows, :] = (total + jnp.concatenate(inside)).astype(BF)
        weighted = (driven * per_head(toend, first, group, width)).astype(BF)
        state[rows, :] = entering * per_head(whole, first, group, width) + dot(weighted, in_t, 1, 1)
    carry[...] = qd_ref[0:channels, :]

    @pl.when(step_at == last)
    def _():
        pack_ref[0:inner, :] = state[...].astype(BF)
        factor = prefix[...]
        high = factor.astype(BF)
        pack_ref[inner : inner + padded, :] = high
        pack_ref[inner + padded : inner + 2 * padded, :] = (factor - high.astype(F32)).astype(BF)


def lane_block(rows):
    return pl.BlockSpec((rows, CHUNK), lambda i: (0, i))


def whole_block(shape):
    return pl.BlockSpec(shape, lambda i: (0,) * len(shape))


def scan(qd, halo, taps, bias, log_rate, skip, info, heads, inner):
    length = qd.shape[1]
    padded = bias.shape[0]
    channels = qd.shape[0] - padded
    steps = length // CHUNK
    return pl.pallas_call(
        functools.partial(scan_kernel, heads, inner),
        grid=(steps,),
        in_specs=[
            lane_block(qd.shape[0]),
            whole_block(halo.shape),
            whole_block(taps.shape),
            whole_block(bias.shape),
            whole_block(bias.shape),
            whole_block(bias.shape),
            lane_block(info.shape[0]),
        ],
        out_specs=[
            lane_block(channels),
            lane_block(channels),
            lane_block(inner),
            pl.BlockSpec((1, inner, CHUNK), lambda i: (i, 0, 0)),
            pl.BlockSpec((1, padded, CHUNK), lambda i: (i, 0, 0)),
            lane_block(padded),
            whole_block((inner + 2 * padded, CHUNK)),
        ],
        out_shape=[
            jax.ShapeDtypeStruct((channels, length), BF),
            jax.ShapeDtypeStruct((channels, length), BF),
            jax.ShapeDtypeStruct((inner, length), BF),
            jax.ShapeDtypeStruct((steps, inner, CHUNK), BF),
            jax.ShapeDtypeStruct((steps, padded, CHUNK), F32),
            jax.ShapeDtypeStruct((padded, length), F32),
            jax.ShapeDtypeStruct((inner + 2 * padded, CHUNK), BF),
        ],
        scratch_shapes=[
            pltpu.VMEM((channels, CHUNK), BF),
            pltpu.VMEM((CONV + 1, channels, CHUNK), F32),
            pltpu.VMEM((inner, CHUNK), F32),
            pltpu.VMEM((padded, CHUNK), F32),
        ],
        compiler_params=pltpu.CompilerParams(vmem_limit_bytes=VMEM),
        name="scan_forward",
    )(qd, halo, taps, bias, log_rate, skip, info)


def joined(packs, at, inner, heads, padded):
    width = inner // heads
    first = at // width
    count = CHUNK // width
    total = None
    for pack in reversed(packs):
        own = pack[at : at + CHUNK, :].astype(F32)
        if total is not None:
            high = pack[inner : inner + padded, :].astype(F32)
            low = pack[inner + padded : inner + 2 * padded, :].astype(F32)
            own = own + per_head(high + low, first, count, width) * total
        total = own
    return total


def norm_kernel(heads, n_packs, *refs):
    packs = refs[:n_packs]
    part_ref, z_ref, out_ref, reach_ref, gain_ref, yb_ref, n_ref, enter_ref, value = refs[n_packs:]
    inner = part_ref.shape[0]
    padded = reach_ref.shape[0]
    width = inner // heads
    count = CHUNK // width

    @pl.when(pl.program_id(0) == 0)
    def _():
        for at in range(0, inner, CHUNK):
            if n_packs:
                enter_ref[at : at + CHUNK, :] = joined(packs, at, inner, heads, padded).astype(BF)
            else:
                enter_ref[at : at + CHUNK, :] = jnp.zeros((CHUNK, CHUNK), BF)

    reach = reach_ref[...]
    out_t = out_ref[...]
    squares = jnp.zeros((CHUNK, CHUNK), F32)
    for at in range(0, inner, CHUNK):
        rows = pl.ds(at, CHUNK)
        late = per_head(reach, at // width, count, width) * dot(enter_ref[rows, :], out_t, 1, 0)
        mixed = (part_ref[rows, :].astype(F32) + late).astype(BF)
        yb_ref[rows, :] = mixed
        z = z_ref[rows, :].astype(F32)
        gated = mixed.astype(F32) * (z * sigmoid(z))
        value[rows, :] = gated
        squares = squares + gated * gated
    scale = lax.rsqrt(col_sum(squares) * (1.0 / inner) + EPS)
    for at in range(0, inner, CHUNK):
        rows = pl.ds(at, CHUNK)
        n_ref[rows, :] = (value[rows, :] * scale * gain_ref[rows, :]).astype(BF)


def gated_norm(packs, part, z, xa, reach, gain, heads):
    inner, length = part.shape
    channels = xa.shape[0]
    n_state = (channels - inner) // 2
    out_at = (channels - n_state) // n_state
    return pl.pallas_call(
        functools.partial(norm_kernel, heads, len(packs)),
        grid=(length // CHUNK,),
        in_specs=[whole_block(pack.shape) for pack in packs]
        + [
            lane_block(inner),
            lane_block(inner),
            pl.BlockSpec((n_state, CHUNK), lambda i: (out_at, i)),
            lane_block(reach.shape[0]),
            whole_block(gain.shape),
        ],
        out_specs=[lane_block(inner), lane_block(inner), whole_block((inner, n_state))],
        out_shape=[
            jax.ShapeDtypeStruct((inner, length), BF),
            jax.ShapeDtypeStruct((inner, length), BF),
            jax.ShapeDtypeStruct((inner, n_state), BF),
        ],
        scratch_shapes=[pltpu.VMEM((inner, CHUNK), F32)],
        compiler_params=pltpu.CompilerParams(vmem_limit_bytes=VMEM),
        name="gated_norm_forward",
    )(*packs, part, z, xa, reach, gain)


def norm_back_kernel(
    heads,
    go_ref,
    weight_ref,
    yb_ref,
    z_ref,
    out_ref,
    reach_ref,
    gain_ref,
    pack_in_ref,
    dy_ref,
    dz_ref,
    dgain_ref,
    pack_ref,
    value,
    dn,
    dgain,
    adjoint,
):
    step_at = pl.program_id(0)
    last = pl.num_programs(0) - 1
    inner = yb_ref.shape[0]
    padded = reach_ref.shape[0]
    width = inner // heads
    count = CHUNK // width

    @pl.when(step_at == 0)
    def _():
        dgain[...] = jnp.zeros_like(dgain)
        adjoint[...] = jnp.zeros_like(adjoint)

    go = go_ref[...]
    squares = jnp.zeros((CHUNK, CHUNK), F32)
    crosses = jnp.zeros((CHUNK, CHUNK), F32)
    for at in range(0, inner, CHUNK):
        rows = pl.ds(at, CHUNK)
        d_norm = dot(weight_ref[rows, :], go, 1, 0)
        z = z_ref[rows, :].astype(F32)
        gated = yb_ref[rows, :].astype(F32) * (z * sigmoid(z))
        dn[rows, :] = d_norm
        value[rows, :] = gated
        squares = squares + gated * gated
        crosses = crosses + gated * (d_norm * gain_ref[rows, :])
    scale = lax.rsqrt(col_sum(squares) * (1.0 / inner) + EPS)
    pull = col_sum(crosses) * (1.0 / inner) * scale * scale * scale
    reach = reach_ref[...]
    out_t = out_ref[...]
    for at in range(0, inner, CHUNK):
        rows = pl.ds(at, CHUNK)
        gated = value[rows, :]
        d_norm = dn[rows, :]
        dgain[rows, :] += d_norm * gated * scale
        d_gated = d_norm * gain_ref[rows, :] * scale - gated * pull
        z = z_ref[rows, :].astype(F32)
        gate = sigmoid(z)
        dy = (d_gated * (z * gate)).astype(BF)
        dy_ref[rows, :] = dy
        d_silu = d_gated * yb_ref[rows, :].astype(F32)
        dz_ref[rows, :] = (d_silu * (gate * (1.0 + z * (1.0 - gate)))).astype(BF)
        far = (dy.astype(F32) * per_head(reach, at // width, count, width)).astype(BF)
        adjoint[rows, :] += dot(far, out_t, 1, 1)

    @pl.when(step_at == last)
    def _():
        pack_ref[0:inner, :] = adjoint[...].astype(BF)
        pack_ref[inner : inner + 2 * padded, :] = pack_in_ref[inner : inner + 2 * padded, :]
        for at in range(0, inner, CHUNK):
            dgain_ref[at : at + CHUNK, :] = jnp.sum(
                dgain[at : at + CHUNK, :], axis=1, keepdims=True
            )


def gated_norm_back(go, weight, yb, z, xa, reach, gain, pack, heads):
    inner, length = yb.shape
    channels = xa.shape[0]
    n_state = (channels - inner) // 2
    out_at = (channels - n_state) // n_state
    return pl.pallas_call(
        functools.partial(norm_back_kernel, heads),
        grid=(length // CHUNK,),
        in_specs=[
            lane_block(go.shape[0]),
            whole_block(weight.shape),
            lane_block(inner),
            lane_block(inner),
            pl.BlockSpec((n_state, CHUNK), lambda i: (out_at, i)),
            lane_block(reach.shape[0]),
            whole_block(gain.shape),
            whole_block(pack.shape),
        ],
        out_specs=[
            lane_block(inner),
            lane_block(inner),
            whole_block((inner, 1)),
            whole_block(pack.shape),
        ],
        out_shape=[
            jax.ShapeDtypeStruct((inner, length), BF),
            jax.ShapeDtypeStruct((inner, length), BF),
            jax.ShapeDtypeStruct((inner, 1), F32),
            jax.ShapeDtypeStruct(pack.shape, BF),
        ],
        scratch_shapes=[
            pltpu.VMEM((inner, CHUNK), F32),
            pltpu.VMEM((inner, CHUNK), F32),
            pltpu.VMEM((inner, CHUNK), F32),
            pltpu.VMEM((inner, CHUNK), F32),
        ],
        compiler_params=pltpu.CompilerParams(vmem_limit_bytes=VMEM),
        name="gated_norm_backward",
    )(go, weight, yb, z, xa, reach, gain, pack)


def scan_back_kernel(heads, n_packs, *refs):
    packs = refs[:n_packs]
    (
        xa_ref,
        slope_ref,
        qd_ref,
        dy_ref,
        enter_ref,
        device_ref,
        prefix_ref,
        taps_ref,
        bias_ref,
        log_ref,
        skip_ref,
        info_ref,
        dqd_ref,
        dconv_ref,
        dhead_ref,
        edge_ref,
        wide,
        adjoint,
        later,
        dtaps,
        dhead,
        far_s,
        far_dy,
        far_g,
        far_x,
        rows_total,
        rows_leave,
        rows_direct,
        rows_skip,
        rows_pass,
        d_scores,
    ) = refs[n_packs:]
    step_at = pl.program_id(0)
    last = pl.num_programs(0) - 1
    channels = xa_ref.shape[0]
    inner = dy_ref.shape[0]
    padded = bias_ref.shape[0]
    n_state = (channels - inner) // 2
    width, group, blocks = shape_of(heads, inner, n_state)

    @pl.when(step_at == 0)
    def _():
        for at in range(0, channels, CHUNK):
            for k in range(CONV):
                wide[k, at : at + CHUNK, :] = jnp.broadcast_to(
                    taps_ref[at : at + CHUNK, k : k + 1], (CHUNK, CHUNK)
                )
        for at in range(0, inner, CHUNK):
            if n_packs:
                adjoint[at : at + CHUNK, :] = joined(packs, at, inner, heads, padded)
            else:
                adjoint[at : at + CHUNK, :] = jnp.zeros((CHUNK, CHUNK), F32)
        later[...] = jnp.zeros_like(later)
        dtaps[...] = jnp.zeros_like(dtaps)
        dhead[...] = jnp.zeros_like(dhead)
        for ref in (rows_total, rows_leave, rows_direct, rows_skip, rows_pass):
            ref[...] = jnp.zeros_like(ref)

    info = info_ref[...]
    raw = qd_ref[channels : channels + padded, :].astype(F32)
    shifted, step, rate, running = step_sizes(raw, bias_ref[...], log_ref[...])
    reach, toend, whole = chunk_factors(running, info)
    column = jnp.transpose(running)
    mask = pair_mask(info)
    skip = skip_ref[...]
    before = prefix_ref[0]
    in_t = xa_ref[inner : inner + n_state, :]
    out_t = xa_ref[inner + n_state :, :]
    scores = dot(in_t, out_t, 0, 0)
    lane = lax.broadcasted_iota(jnp.int32, (CHUNK, CHUNK), 1)

    def conv_back(at, d_active):
        rows = pl.ds(at, CHUNK)
        d_pre = d_active.astype(BF).astype(F32) * slope_ref[rows, :].astype(F32)
        q = qd_ref[rows, :].astype(F32)
        after = later[rows, :]
        dtaps[CONV, rows, :] += d_pre
        dtaps[CONV - 1, rows, :] += d_pre * q
        d_q = wide[CONV - 1, rows, :] * d_pre
        for k in range(1, CONV):
            mixed = jnp.where(lane < k, after, d_pre)
            moved = pltpu.roll(mixed, CHUNK - k, 1) * info[3 + k : 4 + k]
            d_q = d_q + wide[CONV - 1 - k, rows, :] * moved
            dtaps[CONV - 1 - k, rows, :] += moved * q
        later[rows, :] = d_pre
        dqd_ref[rows, :] = d_q.astype(BF)

    d_scores[...] = jnp.zeros_like(d_scores)
    for block in range(blocks):
        at = block * CHUNK
        rows = pl.ds(at, CHUNK)
        first = block * group
        x = xa_ref[rows, :].astype(F32)
        dy_low = dy_ref[rows, :]
        dy = dy_low.astype(F32)
        step_rows = per_head(step, first, group, width)
        entering = enter_ref[0, rows, :].astype(F32) + per_head(
            before, first, group, width
        ) * device_ref[rows, :].astype(F32)
        entering_low = entering.astype(BF)
        leaving = adjoint[rows, :]
        leaving_low = leaving.astype(BF)
        passed = entering * leaving
        driven_low = (x * step_rows).astype(BF)
        driven = driven_low.astype(F32)
        reach_dy = dy * per_head(reach, first, group, width)
        end_driven = driven * per_head(toend, first, group, width)
        far_dy_low = reach_dy.astype(BF)
        far_s[rows, :] = entering_low
        far_dy[rows, :] = far_dy_low
        far_g[rows, :] = leaving_low
        far_x[rows, :] = end_driven.astype(BF)
        far_out = reach_dy * dot(entering_low, out_t, 1, 0)
        far_in = dot(leaving_low, in_t, 1, 0)
        adjoint[rows, :] = leaving * per_head(whole, first, group, width) + dot(
            far_dy_low, out_t, 1, 1
        )
        near = []
        inside = []
        for k in range(group):
            head = first + k
            part = slice(k * width, (k + 1) * width)
            gap = (running[head : head + 1] + mask) - column[:, head : head + 1]
            decay = jnp.exp2(gap)
            mixer = (scores * decay).astype(BF)
            inside.append(dot(driven_low[part], mixer, 1, 0))
            near.append(dot(dy_low[part], mixer, 1, 1))
            d_scores[...] += decay * dot(driven_low[part], dy_low[part], 0, 0)
        near = jnp.concatenate(near)
        totals = dy * jnp.concatenate(inside) - driven * near + far_out
        leaves = end_driven * far_in
        d_driven = near + per_head(toend, first, group, width) * far_in
        direct = x * d_driven
        skips = x * dy
        for k in range(group):
            head = slice(first + k, first + k + 1)
            part = slice(k * width, (k + 1) * width)
            rows_total[head, :] = col_sum(totals[part])
            rows_leave[head, :] = col_sum(leaves[part])
            rows_direct[head, :] = col_sum(direct[part])
            rows_skip[head, :] = col_sum(skips[part])
            rows_pass[head, :] = col_sum(passed[part])
        conv_back(at, step_rows * d_driven + per_head(skip, first, group, width) * dy)
    d_scores_low = d_scores[...].astype(BF)
    d_in = dot(out_t, d_scores_low, 1, 1) + dot(far_g[...], far_x[...], 0, 0)
    d_out = dot(in_t, d_scores_low, 1, 0) + dot(far_s[...], far_dy[...], 0, 0)
    conv_back(inner, d_in)
    conv_back(inner + n_state, d_out)
    down, across = iotas()
    at_or_after = (down >= across).astype(F32)
    ahead = (down < across).astype(F32)
    through = jnp.sum(rows_pass[...], axis=1, keepdims=True) * whole
    d_rate = (
        dot(rows_total[...], at_or_after, 1, 0, HIGH)
        + dot(rows_leave[...], ahead, 1, 0, HIGH)
        + through
    )
    d_step = rows_direct[...] + rate * d_rate
    d_raw = d_step * sigmoid(shifted)
    dqd_ref[channels : channels + padded, :] = d_raw.astype(BF)
    dhead[0] += d_raw
    dhead[1] += d_rate * step * rate
    dhead[2] += rows_skip[...]

    @pl.when(step_at == last)
    def _():
        for k in range(3):
            dhead_ref[:, k : k + 1] = jnp.sum(dhead[k], axis=1, keepdims=True)
        for at in range(0, channels, CHUNK):
            for k in range(CONV + 1):
                dconv_ref[at : at + CHUNK, k : k + 1] = jnp.sum(
                    dtaps[k, at : at + CHUNK, :], axis=1, keepdims=True
                )
            edge_ref[:, at : at + CHUNK] = jnp.transpose(later[at : at + CHUNK, :])[0:8, :]


def scan_back(packs, xa, slope, qd, dy, enter, device, prefix, taps, bias, log_rate, skip, info, heads):
    inner, length = dy.shape
    channels = xa.shape[0]
    padded = bias.shape[0]
    steps = length // CHUNK

    def back(rows):
        return pl.BlockSpec((rows, CHUNK), lambda i: (0, steps - 1 - i))

    def back_three(rows):
        return pl.BlockSpec((1, rows, CHUNK), lambda i: (steps - 1 - i, 0, 0))

    return pl.pallas_call(
        functools.partial(scan_back_kernel, heads, len(packs)),
        grid=(steps,),
        in_specs=[whole_block(pack.shape) for pack in packs]
        + [
            back(channels),
            back(channels),
            back(channels + padded),
            back(inner),
            back_three(inner),
            whole_block(device.shape),
            back_three(padded),
            whole_block(taps.shape),
            whole_block(bias.shape),
            whole_block(bias.shape),
            whole_block(bias.shape),
            back(info.shape[0]),
        ],
        out_specs=[
            back(channels + padded),
            whole_block((channels, 8)),
            whole_block((padded, 8)),
            whole_block((8, channels)),
        ],
        out_shape=[
            jax.ShapeDtypeStruct((channels + padded, length), BF),
            jax.ShapeDtypeStruct((channels, 8), F32),
            jax.ShapeDtypeStruct((padded, 8), F32),
            jax.ShapeDtypeStruct((8, channels), F32),
        ],
        scratch_shapes=[
            pltpu.VMEM((CONV, channels, CHUNK), F32),
            pltpu.VMEM((inner, CHUNK), F32),
            pltpu.VMEM((channels, CHUNK), F32),
            pltpu.VMEM((CONV + 1, channels, CHUNK), F32),
            pltpu.VMEM((3, padded, CHUNK), F32),
            pltpu.VMEM((inner, CHUNK), BF),
            pltpu.VMEM((inner, CHUNK), BF),
            pltpu.VMEM((inner, CHUNK), BF),
            pltpu.VMEM((inner, CHUNK), BF),
        ]
        + [pltpu.VMEM((padded, CHUNK), F32)] * 5
        + [pltpu.VMEM((CHUNK, CHUNK), F32)],
        compiler_params=pltpu.CompilerParams(vmem_limit_bytes=VMEM),
        name="scan_backward",
    )(*packs, xa, slope, qd, dy, enter, device, prefix, taps, bias, log_rate, skip, info)


def edge_kernel(dqd_ref, qd_ref, edge_ref, taps_ref, info_ref, dconv_ref, out_ref, dconv_out_ref):
    channels = taps_ref.shape[0]
    lane = lax.broadcasted_iota(jnp.int32, (CHUNK, CHUNK), 1)
    info = info_ref[...]
    out_ref[...] = dqd_ref[...]
    dconv_out_ref[...] = dconv_ref[...]
    for at in range(0, channels, CHUNK):
        rows = pl.ds(at, CHUNK)
        first = jnp.concatenate([edge_ref[:, at : at + CHUNK], jnp.zeros((CHUNK - 8, CHUNK), F32)])
        d_pre = jnp.transpose(first)
        q = qd_ref[rows, :].astype(F32)
        d_q = dqd_ref[rows, :].astype(F32)
        for k in range(1, CONV):
            moved = pltpu.roll(jnp.where(lane < k, d_pre, 0.0), CHUNK - k, 1) * info[3 + k : 4 + k]
            tap = CONV - 1 - k
            d_q = d_q + taps_ref[rows, tap : tap + 1] * moved
            dconv_out_ref[rows, tap : tap + 1] += jnp.sum(moved * q, axis=1, keepdims=True)
        out_ref[rows, :] = d_q.astype(BF)


def edge_fix(dqd, qd, edge, taps, info, dconv):
    end = dqd.shape[1] // CHUNK - 1

    def final(rows):
        return pl.BlockSpec((rows, CHUNK), lambda i: (0, end))

    return pl.pallas_call(
        edge_kernel,
        grid=(1,),
        in_specs=[
            final(dqd.shape[0]),
            final(qd.shape[0]),
            whole_block(edge.shape),
            whole_block(taps.shape),
            final(info.shape[0]),
            whole_block(dconv.shape),
        ],
        out_specs=[final(dqd.shape[0]), whole_block(dconv.shape)],
        out_shape=[
            jax.ShapeDtypeStruct(dqd.shape, BF),
            jax.ShapeDtypeStruct(dconv.shape, F32),
        ],
        input_output_aliases={0: 0},
        compiler_params=pltpu.CompilerParams(vmem_limit_bytes=VMEM),
        name="edge_gradient",
    )(dqd, qd, edge, taps, info, dconv)


def passed_along(block, axis, distance):
    devices = range(lax.axis_size(axis))
    route = [(i - distance, i) for i in devices if i - distance in devices]
    return lax.ppermute(block, axis, route)


def total_over(value, axis):
    size = lax.axis_size(axis)
    if size & (size - 1):
        return lax.psum(value, axis)
    bit = 1
    while bit < size:
        other = lax.ppermute(value, axis, [(i, i ^ bit) for i in range(size)])
        value = (value.astype(F32) + other.astype(F32)).astype(value.dtype)
        bit *= 2
    return value


def token_info(stream_ids, place, rows):
    length = stream_ids.shape[0]
    margin = CHUNK
    ids = jnp.concatenate(
        [jnp.full((margin,), -1, jnp.int32), stream_ids, jnp.full((margin,), -2, jnp.int32)]
    )
    ids = lax.dynamic_slice_in_dim(ids, place * rows, rows + 2 * margin)
    own = ids[margin : margin + rows]
    lines = [own]
    lines += [(ids[margin - k : margin - k + rows] == own) for k in range(1, CONV)]
    lines += [(ids[margin + k : margin + k + rows] == own) for k in range(1, CONV)]
    by_chunk = own.reshape(-1, CHUNK)
    before = ids[margin - 1 : margin - 1 + rows].reshape(-1, CHUNK)[:, :1]
    end = by_chunk[:, -1:]
    lines += [(by_chunk == before).reshape(-1), (by_chunk == end).reshape(-1)]
    lines += [jnp.broadcast_to(before == end, by_chunk.shape).reshape(-1)]
    lines += [jnp.zeros((rows,), jnp.int32)] * (16 - len(lines))
    return jnp.stack([line.astype(F32) for line in lines])


def body(
    tokens,
    cotangent,
    seg_ids,
    norm_gain,
    in_weight,
    dt_weight,
    conv_weight,
    conv_bias,
    dt_bias,
    a_log,
    skip,
    out_gain,
    out_weight,
):
    layers, part_d, _ = in_weight.shape
    shards = lax.axis_size("shard")
    n_seq = lax.axis_size("seq")
    place = lax.axis_index("seq")
    inner = out_weight.shape[1] * shards
    channels = conv_bias.shape[1] * shards
    heads = dt_weight.shape[2]
    padded = -(-heads // 16) * 16
    rows = tokens.shape[1]
    width_d = tokens.shape[2]
    info = token_info(seg_ids[0], place, rows)

    pieces = [norm_gain, conv_weight.reshape(layers, -1), conv_bias, out_gain]
    small = lax.all_gather(jnp.concatenate(pieces, axis=1), "shard", axis=0)
    ends = [0]
    for piece in pieces:
        ends.append(ends[-1] + piece.shape[1])
    small = [small[:, :, a:b].astype(F32) for a, b in zip(ends[:-1], ends[1:])]
    gains_in = small[0].transpose(1, 0, 2).reshape(layers, -1)
    taps_all = small[1].reshape(shards, layers, CONV, -1).transpose(1, 0, 3, 2)
    taps_all = taps_all.reshape(layers, channels, CONV)
    bias_all = small[2].transpose(1, 0, 2).reshape(layers, channels, 1)
    taps_all = jnp.concatenate(
        [taps_all, bias_all, jnp.zeros((layers, channels, 8 - CONV - 1), F32)], axis=2
    )
    gains_out = small[3].transpose(1, 0, 2).reshape(layers, inner, 1)

    head_values = lax.all_gather(jnp.stack([dt_bias, a_log, skip]), "seq", axis=2, tiled=True)
    head_values = jnp.pad(head_values, ((0, 0), (0, 0), (0, padded - heads)))
    head_values = jnp.broadcast_to(head_values[..., None], head_values.shape + (CHUNK,))

    weights = []
    for layer in range(layers):
        scan_part = jnp.concatenate(
            [
                in_weight[layer, :, inner:],
                dt_weight[layer],
                jnp.zeros((part_d, padded - heads), in_weight.dtype),
            ],
            axis=1,
        )
        weights.append(
            (
                lax.all_gather(scan_part, "shard", axis=0, tiled=True),
                lax.all_gather(in_weight[layer, :, :inner], "shard", axis=0, tiled=True),
                lax.all_gather(out_weight[layer], "shard", axis=0, tiled=True),
            )
        )

    hidden = tokens[0].T.astype(F32)
    saved = []
    for layer in range(layers):
        w_scan, w_gate, w_out = weights[layer]
        taps = taps_all[layer]
        bias, log_rate, skips = (head_values[k, layer] for k in range(3))
        gain_out = gains_out[layer]
        inverse = lax.rsqrt(jnp.mean(hidden * hidden, axis=0, keepdims=True) + EPS)
        normed = (hidden * inverse * gains_in[layer][:, None]).astype(BF)
        halo = dot(normed[:, rows - EDGE :], w_scan, 0, 0).astype(BF)
        halo = passed_along(halo, "seq", 1)
        qd = dot(w_scan, normed, 0, 0).astype(BF)
        xa, slope, part, enter, prefix, reach, pack = scan(
            qd, halo, taps, bias, log_rate, skips, info, heads, inner
        )
        packs = [passed_along(pack, "seq", k) for k in range(1, n_seq)]
        z = dot(w_gate, normed, 0, 0).astype(BF)
        yb, gated, device = gated_norm(packs, part, z, xa, reach, gain_out, heads)
        saved.append((hidden, inverse, normed, qd, xa, slope, enter, prefix, reach, pack, z, yb, gated, device))
        hidden = hidden + dot(w_out, gated, 0, 0)
    activations = hidden.astype(BF).T[None]

    grad = cotangent[0].T.astype(F32)
    results = [None] * layers
    for layer in reversed(range(layers)):
        w_scan, w_gate, w_out = weights[layer]
        taps = taps_all[layer]
        bias, log_rate, skips = (head_values[k, layer] for k in range(3))
        gain_out = gains_out[layer]
        gain_in = gains_in[layer][:, None]
        h_in, inverse, normed, qd, xa, slope, enter, prefix, reach, pack, z, yb, gated, device = saved[layer]
        go = grad.astype(BF)
        dy, dz, d_gain_out, back_pack = gated_norm_back(
            go, w_out, yb, z, xa, reach, gain_out, pack, heads
        )
        back_packs = [passed_along(back_pack, "seq", -k) for k in range(1, n_seq)]
        d_w_out = dot(gated, go, 1, 1).astype(BF)
        d_w_gate = dot(normed, dz, 1, 1).astype(BF)
        share_out = lax.psum_scatter(d_w_out, "shard", scatter_dimension=0, tiled=True)
        share_gate = lax.psum_scatter(d_w_gate, "shard", scatter_dimension=0, tiled=True)
        dqd, d_conv, d_head, edge = scan_back(
            back_packs, xa, slope, qd, dy, enter, device, prefix, taps, bias, log_rate, skips, info, heads
        )
        edge = passed_along(edge, "seq", -1)
        d_normed = dot(w_gate, dz, 1, 0)
        dqd, d_conv = edge_fix(dqd, qd, edge, taps, info, d_conv)
        d_w_scan = dot(normed, dqd, 1, 1).astype(BF)
        share_scan = lax.psum_scatter(d_w_scan, "shard", scatter_dimension=0, tiled=True)
        d_normed = d_normed + dot(w_scan, dqd, 1, 0)
        scaled = d_normed * gain_in
        d_gain_in = jnp.sum(d_normed * h_in * inverse, axis=1)
        along = jnp.mean(scaled * h_in, axis=0, keepdims=True)
        grad = grad + scaled * inverse - h_in * (along * inverse * inverse * inverse)
        shares = tuple(total_over(item, "seq") for item in (share_out, share_gate, share_scan))
        vector = jnp.concatenate(
            [
                d_gain_in,
                d_conv[:, : CONV + 1].T.reshape(-1),
                d_gain_out[:, 0],
                d_head[:heads, :3].T.reshape(-1),
            ]
        )
        results[layer] = (shares, lax.psum(vector, ("seq", "shard")))
    which = lax.axis_index("shard")

    def own(vector, index, count):
        return lax.dynamic_slice_in_dim(vector, index * count, count)

    outs = [[] for _ in range(10)]
    for (share_out, share_gate, share_scan), vector in results:
        share_scan = share_scan.astype(F32)
        at = 0
        outs[0].append(own(vector[:width_d], which, width_d // shards))
        at += width_d
        wide = channels - inner
        outs[1].append(jnp.concatenate([share_gate.astype(F32), share_scan[:, :channels]], axis=1))
        outs[2].append(share_scan[:, channels : channels + heads])
        taps = vector[at : at + CONV * channels].reshape(CONV, channels)
        outs[3].append(lax.dynamic_slice_in_dim(taps, which * (channels // shards), channels // shards, 1))
        at += CONV * channels
        outs[4].append(own(vector[at : at + channels], which, channels // shards))
        at += channels
        gain = vector[at : at + inner]
        at += inner
        for k in range(3):
            outs[5 + k].append(own(vector[at : at + heads], place, heads // n_seq))
            at += heads
        outs[8].append(own(gain, which, inner // shards))
        outs[9].append(share_out.astype(F32))
    return (activations, grad.T[None]) + tuple(jnp.stack(item) for item in outs)


def solution(mesh):
    specs = (
        P(None, "shard"),
        P(None, "shard", None),
        P(None, "shard", None),
        P(None, None, "shard"),
        P(None, "shard"),
        P(None, "seq"),
        P(None, "seq"),
        P(None, "seq"),
        P(None, "shard"),
        P(None, "shard", None),
    )
    spread = P("shard", "seq", None)
    return jax.shard_map(
        body,
        mesh=mesh,
        in_specs=(spread, spread, P("shard", None)) + specs,
        out_specs=(spread, spread) + specs,
        check_vma=False,
    )
```

```python
import functools
import math

import jax
import jax.numpy as jnp
from jax import lax
from jax.experimental import pallas as pl
from jax.experimental.pallas import tpu as pltpu
from jax.sharding import PartitionSpec as P

CONV = 4
EPS = 1e-05
CHUNK = 128
STEP = 256
EDGE = 16
LOG2E = 1.4426950408889634
FAR = -1e30
BF = jnp.bfloat16
F32 = jnp.float32
HIGH = lax.Precision.HIGHEST
VMEM = 56 * 1024 * 1024
HBM_BYTES_PER_US = 3_690_000


def dot(left, right, left_dim, right_dim, precision=None):
    return lax.dot_general(
        left,
        right,
        (((left_dim,), (right_dim,)), ((), ())),
        precision=precision,
        preferred_element_type=F32,
    )


def col_sum(value):
    return jnp.sum(value, axis=0, keepdims=True)


def sigmoid(value):
    return 0.5 * jnp.tanh(0.5 * value) + 0.5


def per_head(rows, first, count, width):
    return jnp.concatenate(
        [jnp.broadcast_to(rows[k : k + 1], (width, rows.shape[1])) for k in range(first, first + count)]
    )


def iotas():
    down = lax.broadcasted_iota(jnp.int32, (CHUNK, CHUNK), 0)
    across = lax.broadcasted_iota(jnp.int32, (CHUNK, CHUNK), 1)
    return down, across


def step_sizes(raw, bias, log_rate):
    shifted = raw + bias
    step = jnp.maximum(shifted, 0.0) + jnp.log1p(jnp.exp(-jnp.abs(shifted)))
    rate = -jnp.exp(log_rate)
    down, across = iotas()
    upto = (down <= across).astype(F32)
    running = dot(step * (rate * LOG2E), upto, 1, 0, HIGH)
    return shifted, step, rate, running


def pair_mask(info):
    down, across = iotas()
    tags = info[0:8]
    column = jnp.transpose(tags)[:, 0:1]
    reaches = (column == info[0:1]) & (down <= across)
    return jnp.where(reaches, 0.0, FAR)


def chunk_factors(running, info):
    total = running[:, CHUNK - 1 : CHUNK]
    reach = jnp.exp2(running) * info[7:8]
    toend = jnp.exp2(total - running) * info[8:9]
    whole = jnp.exp2(jnp.broadcast_to(total, running.shape)) * info[9:10]
    return reach, toend, whole


def column_of(rows_ref, at):
    block = jnp.concatenate([rows_ref[:, at : at + CHUNK], jnp.zeros((CHUNK - 8, CHUNK), F32)])
    return jnp.transpose(block)


def shape_of(heads, inner, state):
    width = inner // heads
    return width, CHUNK // width, inner // CHUNK


def conv_block(cur, prev, taps, bias, info):
    lane = lax.broadcasted_iota(jnp.int32, cur.shape, 1)
    total = bias + taps[CONV - 1] * cur
    for k in range(1, CONV):
        mixed = jnp.where(lane >= CHUNK - k, prev, cur)
        total = total + taps[CONV - 1 - k] * (pltpu.roll(mixed, k, 1) * info[k : k + 1])
    return total


def scan_kernel(
    heads,
    inner,
    qd_ref,
    halo_ref,
    taps_ref,
    bias_ref,
    log_ref,
    skip_ref,
    info_ref,
    xa_ref,
    slope_ref,
    part_ref,
    enter_ref,
    prefix_ref,
    reach_ref,
    pack_ref,
    carry,
    wide,
    state,
    prefix,
):
    step_at = pl.program_id(0)
    last = pl.num_programs(0) - 1
    channels = xa_ref.shape[0]
    padded = bias_ref.shape[0]
    n_state = (channels - inner) // 2
    width, group, blocks = shape_of(heads, inner, n_state)

    @pl.when(step_at == 0)
    def _():
        for at in range(0, channels, CHUNK):
            columns = column_of(taps_ref, at)
            rows = halo_ref[:, at : at + CHUNK].astype(F32)
            rows = jnp.concatenate([jnp.zeros((CHUNK - EDGE, CHUNK), F32), rows])
            carry[at : at + CHUNK, :] = jnp.transpose(rows).astype(BF)
            for k in range(CONV + 1):
                wide[k, at : at + CHUNK, :] = jnp.broadcast_to(columns[:, k : k + 1], (CHUNK, CHUNK))
        state[...] = jnp.zeros_like(state)
        prefix[...] = jnp.ones_like(prefix)

    info = info_ref[...]
    raw = qd_ref[channels : channels + padded, :].astype(F32)
    _, step, _, running = step_sizes(raw, bias_ref[...], log_ref[...])
    reach, toend, whole = chunk_factors(running, info)
    before = prefix[...]
    prefix_ref[0] = before
    reach_ref[...] = before * reach
    prefix[...] = before * whole
    column = jnp.transpose(running)
    mask = pair_mask(info)
    skip = skip_ref[...]

    def active(at):
        rows = pl.ds(at, CHUNK)
        pre = conv_block(
            qd_ref[rows, :].astype(F32),
            carry[rows, :].astype(F32),
            [wide[k, rows, :] for k in range(CONV)],
            wide[CONV, rows, :],
            info,
        )
        gate = sigmoid(pre)
        value = (pre * gate).astype(BF)
        xa_ref[rows, :] = value
        slope_ref[rows, :] = (gate * (1.0 + pre * (1.0 - gate))).astype(BF)
        return value

    in_t = active(inner)
    out_t = active(inner + n_state)
    scores = dot(in_t, out_t, 0, 0)
    for block in range(blocks):
        at = block * CHUNK
        rows = pl.ds(at, CHUNK)
        x = active(at).astype(F32)
        first = block * group
        entering = state[rows, :]
        entering_low = entering.astype(BF)
        enter_ref[0, rows, :] = entering_low
        driven = x * per_head(step, first, group, width)
        total = x * per_head(skip, first, group, width) + per_head(
            reach, first, group, width
        ) * dot(entering_low, out_t, 1, 0)
        driven_low = driven.astype(BF)
        inside = []
        for k in range(group):
            head = first + k
            gap = (running[head : head + 1] + mask) - column[:, head : head + 1]
            mixer = (scores * jnp.exp2(gap)).astype(BF)
            inside.append(dot(driven_low[k * width : (k + 1) * width], mixer, 1, 0))
        part_ref[rows, :] = (total + jnp.concatenate(inside)).astype(BF)
        weighted = (driven * per_head(toend, first, group, width)).astype(BF)
        state[rows, :] = entering * per_head(whole, first, group, width) + dot(weighted, in_t, 1, 1)
    carry[...] = qd_ref[0:channels, :]

    @pl.when(step_at == last)
    def _():
        pack_ref[0:inner, :] = state[...].astype(BF)
        factor = prefix[...]
        high = factor.astype(BF)
        pack_ref[inner : inner + padded, :] = high
        pack_ref[inner + padded : inner + 2 * padded, :] = (factor - high.astype(F32)).astype(BF)


def takes(microseconds):
    return pl.CostEstimate(
        flops=0, transcendentals=0, bytes_accessed=int(microseconds * HBM_BYTES_PER_US)
    )


def lane_block(rows, lanes=CHUNK):
    return pl.BlockSpec((rows, lanes), lambda i: (0, i))


def whole_block(shape):
    return pl.BlockSpec(shape, lambda i: (0,) * len(shape))


def scan(qd, halo, taps, bias, log_rate, skip, info, heads, inner):
    length = qd.shape[1]
    padded = bias.shape[0]
    channels = qd.shape[0] - padded
    steps = length // CHUNK
    return pl.pallas_call(
        functools.partial(scan_kernel, heads, inner),
        grid=(steps,),
        in_specs=[
            lane_block(qd.shape[0]),
            whole_block(halo.shape),
            whole_block(taps.shape),
            whole_block(bias.shape),
            whole_block(bias.shape),
            whole_block(bias.shape),
            lane_block(info.shape[0]),
        ],
        out_specs=[
            lane_block(channels),
            lane_block(channels),
            lane_block(inner),
            pl.BlockSpec((1, inner, CHUNK), lambda i: (i, 0, 0)),
            pl.BlockSpec((1, padded, CHUNK), lambda i: (i, 0, 0)),
            lane_block(padded),
            whole_block((inner + 2 * padded, CHUNK)),
        ],
        out_shape=[
            jax.ShapeDtypeStruct((channels, length), BF),
            jax.ShapeDtypeStruct((channels, length), BF),
            jax.ShapeDtypeStruct((inner, length), BF),
            jax.ShapeDtypeStruct((steps, inner, CHUNK), BF),
            jax.ShapeDtypeStruct((steps, padded, CHUNK), F32),
            jax.ShapeDtypeStruct((padded, length), F32),
            jax.ShapeDtypeStruct((inner + 2 * padded, CHUNK), BF),
        ],
        scratch_shapes=[
            pltpu.VMEM((channels, CHUNK), BF),
            pltpu.VMEM((CONV + 1, channels, CHUNK), F32),
            pltpu.VMEM((inner, CHUNK), F32),
            pltpu.VMEM((padded, CHUNK), F32),
        ],
        compiler_params=pltpu.CompilerParams(vmem_limit_bytes=VMEM),
        cost_estimate=takes(20),
        name="scan_forward",
    )(qd, halo, taps, bias, log_rate, skip, info)


def joined(packs, at, inner, heads, padded):
    width = inner // heads
    first = at // width
    count = CHUNK // width
    total = None
    for pack in reversed(packs):
        own = pack[at : at + CHUNK, :].astype(F32)
        if total is not None:
            high = pack[inner : inner + padded, :].astype(F32)
            low = pack[inner + padded : inner + 2 * padded, :].astype(F32)
            own = own + per_head(high + low, first, count, width) * total
        total = own
    return total


def norm_kernel(heads, n_packs, *refs):
    packs = refs[:n_packs]
    part_ref, z_ref, out_ref, reach_ref, gain_ref, yb_ref, n_ref, enter_ref, value, gain = refs[n_packs:]
    inner = part_ref.shape[0]
    padded = reach_ref.shape[0]
    width = inner // heads
    count = CHUNK // width

    @pl.when(pl.program_id(0) == 0)
    def _():
        for at in range(0, inner, CHUNK):
            gain[at : at + CHUNK, :] = column_of(gain_ref, at)[:, 0:1]
            if n_packs:
                enter_ref[at : at + CHUNK, :] = joined(packs, at, inner, heads, padded).astype(BF)
            else:
                enter_ref[at : at + CHUNK, :] = jnp.zeros((CHUNK, CHUNK), BF)

    reach = reach_ref[...]
    value[...] = dot(enter_ref[...], out_ref[...], 1, 0)
    squares = jnp.zeros((CHUNK, reach.shape[1]), F32)
    for at in range(0, inner, CHUNK):
        rows = pl.ds(at, CHUNK)
        late = per_head(reach, at // width, count, width) * value[rows, :]
        mixed = (part_ref[rows, :].astype(F32) + late).astype(BF)
        yb_ref[rows, :] = mixed
        z = z_ref[rows, :].astype(F32)
        gated = mixed.astype(F32) * (z * sigmoid(z))
        value[rows, :] = gated
        squares = squares + gated * gated
    scale = lax.rsqrt(col_sum(squares) * (1.0 / inner) + EPS)
    for at in range(0, inner, CHUNK):
        rows = pl.ds(at, CHUNK)
        n_ref[rows, :] = (value[rows, :] * scale * gain[rows, :]).astype(BF)


def gated_norm(packs, part, z, xa, reach, gain, heads):
    inner, length = part.shape
    lanes = math.gcd(length, STEP)
    channels = xa.shape[0]
    n_state = (channels - inner) // 2
    out_at = (channels - n_state) // n_state
    return pl.pallas_call(
        functools.partial(norm_kernel, heads, len(packs)),
        grid=(length // lanes,),
        in_specs=[whole_block(pack.shape) for pack in packs]
        + [
            lane_block(inner, lanes),
            lane_block(inner, lanes),
            pl.BlockSpec((n_state, lanes), lambda i: (out_at, i)),
            lane_block(reach.shape[0], lanes),
            whole_block(gain.shape),
        ],
        out_specs=[lane_block(inner, lanes), lane_block(inner, lanes), whole_block((inner, n_state))],
        out_shape=[
            jax.ShapeDtypeStruct((inner, length), BF),
            jax.ShapeDtypeStruct((inner, length), BF),
            jax.ShapeDtypeStruct((inner, n_state), BF),
        ],
        scratch_shapes=[pltpu.VMEM((inner, lanes), F32), pltpu.VMEM((inner, 1), F32)],
        compiler_params=pltpu.CompilerParams(vmem_limit_bytes=VMEM),
        cost_estimate=takes(9),
        name="gated_norm_forward",
    )(*packs, part, z, xa, reach, gain)


def norm_back_kernel(heads, n_after, *refs):
    norm_back_step(heads, *refs[n_after:])


def norm_back_step(
    heads,
    go_ref,
    weight_ref,
    yb_ref,
    z_ref,
    out_ref,
    reach_ref,
    gain_ref,
    pack_in_ref,
    dy_ref,
    dz_ref,
    dgain_ref,
    pack_ref,
    value,
    dn,
    dgain,
    adjoint,
    far,
    gain,
):
    step_at = pl.program_id(0)
    last = pl.num_programs(0) - 1
    inner = yb_ref.shape[0]
    padded = reach_ref.shape[0]
    width = inner // heads
    count = CHUNK // width

    @pl.when(step_at == 0)
    def _():
        for at in range(0, inner, CHUNK):
            gain[at : at + CHUNK, :] = column_of(gain_ref, at)[:, 0:1]
        dgain[...] = jnp.zeros_like(dgain)
        adjoint[...] = jnp.zeros_like(adjoint)

    go = go_ref[...]
    dn[...] = dot(weight_ref[...], go, 1, 0)
    squares = jnp.zeros((CHUNK, go.shape[1]), F32)
    crosses = jnp.zeros((CHUNK, go.shape[1]), F32)
    for at in range(0, inner, CHUNK):
        rows = pl.ds(at, CHUNK)
        d_norm = dn[rows, :]
        z = z_ref[rows, :].astype(F32)
        gated = yb_ref[rows, :].astype(F32) * (z * sigmoid(z))
        value[rows, :] = gated
        squares = squares + gated * gated
        crosses = crosses + gated * (d_norm * gain[rows, :])
    scale = lax.rsqrt(col_sum(squares) * (1.0 / inner) + EPS)
    pull = col_sum(crosses) * (1.0 / inner) * scale * scale * scale
    reach = reach_ref[...]
    for at in range(0, inner, CHUNK):
        rows = pl.ds(at, CHUNK)
        gated = value[rows, :]
        d_norm = dn[rows, :]
        dgain[rows, :] += d_norm * gated * scale
        d_gated = d_norm * gain[rows, :] * scale - gated * pull
        z = z_ref[rows, :].astype(F32)
        gate = sigmoid(z)
        dy = (d_gated * (z * gate)).astype(BF)
        dy_ref[rows, :] = dy
        d_silu = d_gated * yb_ref[rows, :].astype(F32)
        dz_ref[rows, :] = (d_silu * (gate * (1.0 + z * (1.0 - gate)))).astype(BF)
        far[rows, :] = (dy.astype(F32) * per_head(reach, at // width, count, width)).astype(BF)
    adjoint[...] += dot(far[...], out_ref[...], 1, 1)

    @pl.when(step_at == last)
    def _():
        pack_ref[0:inner, :] = adjoint[...].astype(BF)
        pack_ref[inner : inner + 2 * padded, :] = pack_in_ref[inner : inner + 2 * padded, :]
        for at in range(0, inner, CHUNK):
            total = jnp.sum(dgain[at : at + CHUNK, :], axis=1, keepdims=True)
            total = jnp.transpose(jnp.broadcast_to(total, (CHUNK, CHUNK)))
            dgain_ref[:, at : at + CHUNK] = total[0:8]


def gated_norm_back(go, weight, yb, z, xa, reach, gain, pack, heads, after):
    inner, length = yb.shape
    lanes = math.gcd(length, STEP)
    channels = xa.shape[0]
    n_state = (channels - inner) // 2
    out_at = (channels - n_state) // n_state
    return pl.pallas_call(
        functools.partial(norm_back_kernel, heads, len(after)),
        grid=(length // lanes,),
        in_specs=[pl.BlockSpec(memory_space=pl.ANY)] * len(after)
        + [
            lane_block(go.shape[0], lanes),
            whole_block(weight.shape),
            lane_block(inner, lanes),
            lane_block(inner, lanes),
            pl.BlockSpec((n_state, lanes), lambda i: (out_at, i)),
            lane_block(reach.shape[0], lanes),
            whole_block(gain.shape),
            whole_block(pack.shape),
        ],
        out_specs=[
            lane_block(inner, lanes),
            lane_block(inner, lanes),
            whole_block((8, inner)),
            whole_block(pack.shape),
        ],
        out_shape=[
            jax.ShapeDtypeStruct((inner, length), BF),
            jax.ShapeDtypeStruct((inner, length), BF),
            jax.ShapeDtypeStruct((8, inner), F32),
            jax.ShapeDtypeStruct(pack.shape, BF),
        ],
        scratch_shapes=[
            pltpu.VMEM((inner, lanes), F32),
            pltpu.VMEM((inner, lanes), F32),
            pltpu.VMEM((inner, lanes), F32),
            pltpu.VMEM((inner, n_state), F32),
            pltpu.VMEM((inner, lanes), BF),
            pltpu.VMEM((inner, 1), F32),
        ],
        compiler_params=pltpu.CompilerParams(vmem_limit_bytes=VMEM),
        cost_estimate=takes(17),
        name="gated_norm_backward",
    )(*after, go, weight, yb, z, xa, reach, gain, pack)


def scan_back_kernel(heads, n_packs, n_after, *refs):
    packs = refs[:n_packs]
    (
        xa_ref,
        slope_ref,
        qd_ref,
        dy_ref,
        enter_ref,
        device_ref,
        prefix_ref,
        taps_ref,
        bias_ref,
        log_ref,
        skip_ref,
        info_ref,
        dqd_ref,
        dconv_ref,
        dhead_ref,
        edge_ref,
        wide,
        adjoint,
        later,
        dtaps,
        dhead,
        far_s,
        far_dy,
        far_g,
        far_x,
        rows_total,
        rows_leave,
        rows_direct,
        rows_skip,
        rows_pass,
        d_scores,
    ) = refs[n_packs + n_after :]
    step_at = pl.program_id(0)
    last = pl.num_programs(0) - 1
    channels = xa_ref.shape[0]
    inner = dy_ref.shape[0]
    padded = bias_ref.shape[0]
    n_state = (channels - inner) // 2
    width, group, blocks = shape_of(heads, inner, n_state)

    @pl.when(step_at == 0)
    def _():
        for at in range(0, channels, CHUNK):
            columns = column_of(taps_ref, at)
            for k in range(CONV):
                wide[k, at : at + CHUNK, :] = jnp.broadcast_to(columns[:, k : k + 1], (CHUNK, CHUNK))
        for at in range(0, inner, CHUNK):
            if n_packs:
                adjoint[at : at + CHUNK, :] = joined(packs, at, inner, heads, padded)
            else:
                adjoint[at : at + CHUNK, :] = jnp.zeros((CHUNK, CHUNK), F32)
        later[...] = jnp.zeros_like(later)
        dtaps[...] = jnp.zeros_like(dtaps)
        dhead[...] = jnp.zeros_like(dhead)
        for ref in (rows_total, rows_leave, rows_direct, rows_skip, rows_pass):
            ref[...] = jnp.zeros_like(ref)

    info = info_ref[...]
    raw = qd_ref[channels : channels + padded, :].astype(F32)
    shifted, step, rate, running = step_sizes(raw, bias_ref[...], log_ref[...])
    reach, toend, whole = chunk_factors(running, info)
    column = jnp.transpose(running)
    mask = pair_mask(info)
    skip = skip_ref[...]
    before = prefix_ref[0]
    in_t = xa_ref[inner : inner + n_state, :]
    out_t = xa_ref[inner + n_state :, :]
    scores = dot(in_t, out_t, 0, 0)
    lane = lax.broadcasted_iota(jnp.int32, (CHUNK, CHUNK), 1)

    def conv_back(at, d_active):
        rows = pl.ds(at, CHUNK)
        d_pre = d_active.astype(BF).astype(F32) * slope_ref[rows, :].astype(F32)
        q = qd_ref[rows, :].astype(F32)
        after = later[rows, :]
        dtaps[CONV, rows, :] += d_pre
        dtaps[CONV - 1, rows, :] += d_pre * q
        d_q = wide[CONV - 1, rows, :] * d_pre
        for k in range(1, CONV):
            mixed = jnp.where(lane < k, after, d_pre)
            moved = pltpu.roll(mixed, CHUNK - k, 1) * info[3 + k : 4 + k]
            d_q = d_q + wide[CONV - 1 - k, rows, :] * moved
            dtaps[CONV - 1 - k, rows, :] += moved * q
        later[rows, :] = d_pre
        dqd_ref[rows, :] = d_q.astype(BF)

    d_scores[...] = jnp.zeros_like(d_scores)
    for block in range(blocks):
        at = block * CHUNK
        rows = pl.ds(at, CHUNK)
        first = block * group
        x = xa_ref[rows, :].astype(F32)
        dy_low = dy_ref[rows, :]
        dy = dy_low.astype(F32)
        step_rows = per_head(step, first, group, width)
        entering = enter_ref[0, rows, :].astype(F32) + per_head(
            before, first, group, width
        ) * device_ref[rows, :].astype(F32)
        entering_low = entering.astype(BF)
        leaving = adjoint[rows, :]
        leaving_low = leaving.astype(BF)
        passed = entering * leaving
        driven_low = (x * step_rows).astype(BF)
        driven = driven_low.astype(F32)
        reach_dy = dy * per_head(reach, first, group, width)
        end_driven = driven * per_head(toend, first, group, width)
        far_dy_low = reach_dy.astype(BF)
        far_s[rows, :] = entering_low
        far_dy[rows, :] = far_dy_low
        far_g[rows, :] = leaving_low
        far_x[rows, :] = end_driven.astype(BF)
        far_out = reach_dy * dot(entering_low, out_t, 1, 0)
        far_in = dot(leaving_low, in_t, 1, 0)
        adjoint[rows, :] = leaving * per_head(whole, first, group, width) + dot(
            far_dy_low, out_t, 1, 1
        )
        near = []
        inside = []
        for k in range(group):
            head = first + k
            part = slice(k * width, (k + 1) * width)
            gap = (running[head : head + 1] + mask) - column[:, head : head + 1]
            decay = jnp.exp2(gap)
            mixer = (scores * decay).astype(BF)
            inside.append(dot(driven_low[part], mixer, 1, 0))
            near.append(dot(dy_low[part], mixer, 1, 1))
            d_scores[...] += decay * dot(driven_low[part], dy_low[part], 0, 0)
        near = jnp.concatenate(near)
        totals = dy * jnp.concatenate(inside) - driven * near + far_out
        leaves = end_driven * far_in
        d_driven = near + per_head(toend, first, group, width) * far_in
        direct = x * d_driven
        skips = x * dy
        for k in range(group):
            head = slice(first + k, first + k + 1)
            part = slice(k * width, (k + 1) * width)
            rows_total[head, :] = col_sum(totals[part])
            rows_leave[head, :] = col_sum(leaves[part])
            rows_direct[head, :] = col_sum(direct[part])
            rows_skip[head, :] = col_sum(skips[part])
            rows_pass[head, :] = col_sum(passed[part])
        conv_back(at, step_rows * d_driven + per_head(skip, first, group, width) * dy)
    d_scores_low = d_scores[...].astype(BF)
    d_in = dot(out_t, d_scores_low, 1, 1) + dot(far_g[...], far_x[...], 0, 0)
    d_out = dot(in_t, d_scores_low, 1, 0) + dot(far_s[...], far_dy[...], 0, 0)
    conv_back(inner, d_in)
    conv_back(inner + n_state, d_out)
    down, across = iotas()
    at_or_after = (down >= across).astype(F32)
    ahead = (down < across).astype(F32)
    through = jnp.sum(rows_pass[...], axis=1, keepdims=True) * whole
    d_rate = (
        dot(rows_total[...], at_or_after, 1, 0, HIGH)
        + dot(rows_leave[...], ahead, 1, 0, HIGH)
        + through
    )
    d_step = rows_direct[...] + rate * d_rate
    d_raw = d_step * sigmoid(shifted)
    dqd_ref[channels : channels + padded, :] = d_raw.astype(BF)
    dhead[0] += d_raw
    dhead[1] += d_rate * step * rate
    dhead[2] += rows_skip[...]

    @pl.when(step_at == last)
    def _():
        for k in range(3):
            dhead_ref[:, k : k + 1] = jnp.sum(dhead[k], axis=1, keepdims=True)
        for at in range(0, channels, CHUNK):
            totals = jnp.zeros((CHUNK, CHUNK), F32)
            for k in range(CONV + 1):
                one = jnp.sum(dtaps[k, at : at + CHUNK, :], axis=1, keepdims=True)
                totals = jnp.where(lane == k, one, totals)
            dconv_ref[:, at : at + CHUNK] = jnp.transpose(totals)[0:8]
            edge_ref[:, at : at + CHUNK] = jnp.transpose(later[at : at + CHUNK, :])[0:8, :]


def scan_back(packs, xa, slope, qd, dy, enter, device, prefix, taps, bias, log_rate, skip, info, heads, after):
    inner, length = dy.shape
    channels = xa.shape[0]
    padded = bias.shape[0]
    steps = length // CHUNK

    def back(rows):
        return pl.BlockSpec((rows, CHUNK), lambda i: (0, steps - 1 - i))

    def back_three(rows):
        return pl.BlockSpec((1, rows, CHUNK), lambda i: (steps - 1 - i, 0, 0))

    return pl.pallas_call(
        functools.partial(scan_back_kernel, heads, len(packs), len(after)),
        grid=(steps,),
        in_specs=[whole_block(pack.shape) for pack in packs]
        + [pl.BlockSpec(memory_space=pl.ANY)] * len(after)
        + [
            back(channels),
            back(channels),
            back(channels + padded),
            back(inner),
            back_three(inner),
            whole_block(device.shape),
            back_three(padded),
            whole_block(taps.shape),
            whole_block(bias.shape),
            whole_block(bias.shape),
            whole_block(bias.shape),
            back(info.shape[0]),
        ],
        out_specs=[
            back(channels + padded),
            whole_block((8, channels)),
            whole_block((padded, 8)),
            whole_block((8, channels)),
        ],
        out_shape=[
            jax.ShapeDtypeStruct((channels + padded, length), BF),
            jax.ShapeDtypeStruct((8, channels), F32),
            jax.ShapeDtypeStruct((padded, 8), F32),
            jax.ShapeDtypeStruct((8, channels), F32),
        ],
        scratch_shapes=[
            pltpu.VMEM((CONV, channels, CHUNK), F32),
            pltpu.VMEM((inner, CHUNK), F32),
            pltpu.VMEM((channels, CHUNK), F32),
            pltpu.VMEM((CONV + 1, channels, CHUNK), F32),
            pltpu.VMEM((3, padded, CHUNK), F32),
            pltpu.VMEM((inner, CHUNK), BF),
            pltpu.VMEM((inner, CHUNK), BF),
            pltpu.VMEM((inner, CHUNK), BF),
            pltpu.VMEM((inner, CHUNK), BF),
        ]
        + [pltpu.VMEM((padded, CHUNK), F32)] * 5
        + [pltpu.VMEM((CHUNK, CHUNK), F32)],
        compiler_params=pltpu.CompilerParams(vmem_limit_bytes=VMEM),
        cost_estimate=takes(33),
        name="scan_backward",
    )(*packs, *after, xa, slope, qd, dy, enter, device, prefix, taps, bias, log_rate, skip, info)


def edge_kernel(n_after, dqd_ref, fix_ref, *refs):
    out_ref = refs[n_after]
    channels = fix_ref.shape[1]
    out_ref[...] = dqd_ref[...]
    for at in range(0, channels, CHUNK):
        rows = pl.ds(at, CHUNK)
        fix = jnp.concatenate(
            [jnp.zeros((CHUNK - 8, CHUNK), F32), fix_ref[:, at : at + CHUNK]]
        )
        out_ref[rows, :] = (dqd_ref[rows, :].astype(F32) + jnp.transpose(fix)).astype(BF)


def edge_fix(dqd, fix, after):
    end = dqd.shape[1] // CHUNK - 1
    block = pl.BlockSpec((dqd.shape[0], CHUNK), lambda i: (0, end))
    return pl.pallas_call(
        functools.partial(edge_kernel, len(after)),
        grid=(1,),
        in_specs=[block, whole_block(fix.shape)] + [pl.BlockSpec(memory_space=pl.ANY)] * len(after),
        out_specs=block,
        out_shape=jax.ShapeDtypeStruct(dqd.shape, BF),
        input_output_aliases={0: 0},
        compiler_params=pltpu.CompilerParams(vmem_limit_bytes=VMEM),
        cost_estimate=takes(2),
        name="edge_gradient",
    )(dqd, fix, *after)


def edge_terms(edge, last_q, taps, info):
    rows = edge.shape[0]
    moved = []
    for k in range(1, CONV):
        below = jnp.concatenate([jnp.zeros((rows - k, edge.shape[1]), F32), edge[:k]])
        moved.append(below * info[3 + k, -rows:][:, None])
    fix = sum(taps[CONV - 1 - k][None, :] * moved[k - 1] for k in range(1, CONV))
    d_taps = [jnp.sum(moved[k - 1] * last_q, axis=0) for k in range(CONV - 1, 0, -1)]
    return fix, jnp.stack(d_taps)


def passed_along(block, axis, distance):
    devices = range(lax.axis_size(axis))
    route = [(i - distance, i) for i in devices if i - distance in devices]
    return lax.ppermute(block, axis, route)


def total_over(value, axis):
    size = lax.axis_size(axis)
    if size & (size - 1):
        return jnp.sum(lax.all_gather(value, axis).astype(F32), axis=0)
    terms = [value] + [
        lax.ppermute(value, axis, [(i, i ^ k) for i in range(size)]) for k in range(1, size)
    ]
    terms = [term.astype(F32) for term in terms]
    while len(terms) > 1:
        terms = [terms[k] + terms[k + 1] for k in range(0, len(terms), 2)]
    return terms[0]


def split_total_over(value, axis):
    size = lax.axis_size(axis)
    if size & (size - 1) or value.shape[0] % size:
        return lax.psum(value, axis)
    me = lax.axis_index(axis)
    parts = value.reshape((size, -1) + value.shape[1:])

    def swap(item, k):
        return lax.ppermute(item, axis, [(i, i ^ k) for i in range(size)])

    total = lax.dynamic_index_in_dim(parts, me, keepdims=False).astype(F32)
    for k in range(1, size):
        total = total + swap(lax.dynamic_index_in_dim(parts, me ^ k, keepdims=False), k).astype(F32)
    total = total.astype(value.dtype)
    for k in range(size):
        item = swap(total, k) if k else total
        parts = lax.dynamic_update_index_in_dim(parts, item, me ^ k, 0)
    return parts.reshape(value.shape)


def doubled(value, axis):
    size = lax.axis_size(axis)
    if size & (size - 1):
        return jnp.sum(lax.all_gather(value, axis), axis=0)
    bit = 1
    while bit < size:
        value = value + lax.ppermute(value, axis, [(i, i ^ bit) for i in range(size)])
        bit *= 2
    return value


def token_info(stream_ids, place, rows):
    length = stream_ids.shape[0]
    margin = CHUNK
    ids = jnp.concatenate(
        [jnp.full((margin,), -1, jnp.int32), stream_ids, jnp.full((margin,), -2, jnp.int32)]
    )
    ids = lax.dynamic_slice_in_dim(ids, place * rows, rows + 2 * margin)
    own = ids[margin : margin + rows]
    lines = [own]
    lines += [(ids[margin - k : margin - k + rows] == own) for k in range(1, CONV)]
    lines += [(ids[margin + k : margin + k + rows] == own) for k in range(1, CONV)]
    by_chunk = own.reshape(-1, CHUNK)
    before = ids[margin - 1 : margin - 1 + rows].reshape(-1, CHUNK)[:, :1]
    end = by_chunk[:, -1:]
    lines += [(by_chunk == before).reshape(-1), (by_chunk == end).reshape(-1)]
    lines += [jnp.broadcast_to(before == end, by_chunk.shape).reshape(-1)]
    lines += [jnp.zeros((rows,), jnp.int32)] * (16 - len(lines))
    return jnp.stack([line.astype(F32) for line in lines])


def body(
    tokens,
    cotangent,
    seg_ids,
    norm_gain,
    in_weight,
    dt_weight,
    conv_weight,
    conv_bias,
    dt_bias,
    a_log,
    skip,
    out_gain,
    out_weight,
):
    layers, part_d, _ = in_weight.shape
    shards = lax.axis_size("shard")
    n_seq = lax.axis_size("seq")
    place = lax.axis_index("seq")
    inner = out_weight.shape[1] * shards
    channels = conv_bias.shape[1] * shards
    heads = dt_weight.shape[2]
    padded = -(-heads // 16) * 16
    rows = tokens.shape[1]
    width_d = tokens.shape[2]
    info = token_info(seg_ids[0], place, rows)

    pieces = [norm_gain, conv_weight.reshape(layers, -1), conv_bias, out_gain]
    small = lax.all_gather(jnp.concatenate(pieces, axis=1), "shard", axis=0)
    ends = [0]
    for piece in pieces:
        ends.append(ends[-1] + piece.shape[1])
    small = [small[:, :, a:b].astype(F32) for a, b in zip(ends[:-1], ends[1:])]
    gains_in = small[0].transpose(1, 0, 2).reshape(layers, -1)
    taps_all = small[1].reshape(shards, layers, CONV, -1).transpose(1, 2, 0, 3)
    taps_all = taps_all.reshape(layers, CONV, channels)
    bias_all = small[2].transpose(1, 0, 2).reshape(layers, 1, channels)
    taps_all = jnp.concatenate(
        [taps_all, bias_all, jnp.zeros((layers, 8 - CONV - 1, channels), F32)], axis=1
    )
    gains_out = small[3].transpose(1, 0, 2).reshape(layers, 1, inner)
    gains_out = jnp.broadcast_to(gains_out, (layers, 8, inner))

    head_values = lax.all_gather(jnp.stack([dt_bias, a_log, skip]), "seq", axis=2, tiled=True)
    head_values = jnp.pad(head_values, ((0, 0), (0, 0), (0, padded - heads)))
    head_values = jnp.broadcast_to(head_values[..., None], head_values.shape + (CHUNK,))

    weights = []
    for layer in range(layers):
        scan_part = jnp.concatenate(
            [
                in_weight[layer, :, inner:],
                dt_weight[layer],
                jnp.zeros((part_d, padded - heads), in_weight.dtype),
            ],
            axis=1,
        )
        weights.append(
            (
                lax.all_gather(scan_part, "shard", axis=0, tiled=True),
                lax.all_gather(in_weight[layer, :, :inner], "shard", axis=0, tiled=True),
                lax.all_gather(out_weight[layer], "shard", axis=0, tiled=True),
            )
        )

    hidden = tokens[0].T.astype(F32)
    saved = []
    for layer in range(layers):
        w_scan, w_gate, w_out = weights[layer]
        taps = taps_all[layer]
        bias, log_rate, skips = (head_values[k, layer] for k in range(3))
        gain_out = gains_out[layer]
        inverse = lax.rsqrt(jnp.mean(hidden * hidden, axis=0, keepdims=True) + EPS)
        normed = (hidden * inverse * gains_in[layer][:, None]).astype(BF)
        halo = dot(normed[:, rows - EDGE :], w_scan, 0, 0).astype(BF)
        last_q = halo[EDGE - 8 :, :channels]
        halo = passed_along(halo, "seq", 1)
        qd = dot(w_scan, normed, 0, 0).astype(BF)
        xa, slope, part, enter, prefix, reach, pack = scan(
            qd, halo, taps, bias, log_rate, skips, info, heads, inner
        )
        packs = [passed_along(pack, "seq", k) for k in range(1, n_seq)]
        z = dot(w_gate, normed, 0, 0).astype(BF)
        yb, gated, device = gated_norm(packs, part, z, xa, reach, gain_out, heads)
        saved.append((last_q, hidden, inverse, normed, qd, xa, slope, enter, prefix, reach, pack, z, yb, gated, device))
        hidden = hidden + dot(w_out, gated, 0, 0)
    activations = hidden.astype(BF).T[None]

    grad = cotangent[0].T.astype(F32)
    results = [None] * layers
    before_norm = []
    for layer in reversed(range(layers)):
        w_scan, w_gate, w_out = weights[layer]
        taps = taps_all[layer]
        bias, log_rate, skips = (head_values[k, layer] for k in range(3))
        gain_out = gains_out[layer]
        gain_in = gains_in[layer][:, None]
        last_q, h_in, inverse, normed, qd, xa, slope, enter, prefix, reach, pack, z, yb, gated, device = saved[layer]
        go = grad.astype(BF)
        dy, dz, d_gain_out, back_pack = gated_norm_back(
            go, w_out, yb, z, xa, reach, gain_out, pack, heads, before_norm
        )
        back_packs = [passed_along(back_pack, "seq", -k) for k in range(1, n_seq)]
        d_w_out = dot(gated, go, 1, 1).astype(BF)
        d_w_gate = dot(normed, dz, 1, 1).astype(BF)
        joint = jnp.concatenate(
            [d_w_out.reshape(shards, -1, width_d)]
            + [
                d_w_gate[:, at : at + width_d].reshape(shards, part_d, width_d)
                for at in range(0, inner, width_d)
            ],
            axis=1,
        )
        share_joint = lax.psum_scatter(joint, "shard", scatter_dimension=0, tiled=True)[0]
        d_normed = dot(w_gate, dz, 1, 0)
        dqd, d_conv, d_head, edge = scan_back(
            back_packs, xa, slope, qd, dy, enter, device, prefix, taps, bias, log_rate, skips, info, heads,
            [joint, d_normed],
        )
        edge = passed_along(edge, "seq", -1)
        fix, d_taps = edge_terms(edge, last_q.astype(F32), taps, info)
        dqd = edge_fix(dqd, fix, [])
        d_w_scan = dot(normed, dqd, 1, 1).astype(BF)
        dqd, d_w_scan, share_joint = lax.optimization_barrier((dqd, d_w_scan, share_joint))
        share_scan = lax.psum_scatter(d_w_scan, "shard", scatter_dimension=0, tiled=True)
        d_normed = d_normed + dot(w_scan, dqd, 1, 0)
        scaled = d_normed * gain_in
        d_gain_in = jnp.sum(d_normed * h_in * inverse, axis=1)
        along = jnp.mean(scaled * h_in, axis=0, keepdims=True)
        grad = grad + scaled * inverse - h_in * (along * inverse * inverse * inverse)
        shares = (share_joint, total_over(share_scan, "seq"))
        before_norm = [d_w_scan]
        conv_rows = d_conv[: CONV + 1] + jnp.pad(d_taps, ((0, 2), (0, 0)))
        pieces = [d_gain_in, conv_rows.reshape(-1), d_gain_out[0], d_head[:heads, :3].T.reshape(-1)]
        results[layer] = (shares, pieces)
    joint = jnp.concatenate([shares[0] for shares, _ in results])
    joint = split_total_over(joint, "seq").astype(F32).reshape(layers, -1, width_d)
    small = jnp.concatenate([item for _, pieces in results for item in pieces])
    small = doubled(doubled(small, "shard"), "seq")
    which = lax.axis_index("shard")

    def own(vector, index, count):
        return lax.dynamic_slice_in_dim(vector, index * count, count)

    outs = [[] for _ in range(10)]
    part_i = inner // shards
    part_c = channels // shards
    at = 0
    for share_joint, ((_, share_scan), _) in zip(joint, results):
        share_gate = jnp.concatenate(
            [share_joint[k : k + part_d] for k in range(part_i, share_joint.shape[0], part_d)], axis=1
        )
        outs[0].append(own(small[at : at + width_d], which, part_d))
        at += width_d
        outs[1].append(jnp.concatenate([share_gate, share_scan[:, :channels]], axis=1))
        outs[2].append(share_scan[:, channels : channels + heads])
        taps = small[at : at + CONV * channels].reshape(CONV, channels)
        outs[3].append(lax.dynamic_slice_in_dim(taps, which * part_c, part_c, 1))
        at += CONV * channels
        outs[4].append(own(small[at : at + channels], which, part_c))
        at += channels
        outs[8].append(own(small[at : at + inner], which, part_i))
        at += inner
        for k in range(3):
            outs[5 + k].append(own(small[at : at + heads], place, heads // n_seq))
            at += heads
        outs[9].append(share_joint[:part_i])
    return (activations, grad.T[None]) + tuple(jnp.stack(item) for item in outs)


def solution(mesh):
    specs = (
        P(None, "shard"),
        P(None, "shard", None),
        P(None, "shard", None),
        P(None, None, "shard"),
        P(None, "shard"),
        P(None, "seq"),
        P(None, "seq"),
        P(None, "seq"),
        P(None, "shard"),
        P(None, "shard", None),
    )
    spread = P("shard", "seq", None)
    return jax.shard_map(
        body,
        mesh=mesh,
        in_specs=(spread, spread, P("shard", None)) + specs,
        out_specs=(spread, spread) + specs,
        check_vma=False,
    )
```

```python
import functools
import math

import jax
import jax.numpy as jnp
from jax import lax
from jax.experimental import pallas as pl
from jax.experimental.pallas import tpu as pltpu
from jax.sharding import PartitionSpec as P

CONV = 4
EPS = 1e-05
CHUNK = 128
STEP = 256
EDGE = 16
LOG2E = 1.4426950408889634
FAR = -1e30
BF = jnp.bfloat16
F32 = jnp.float32
HIGH = lax.Precision.HIGHEST
VMEM = 56 * 1024 * 1024
HBM_BYTES_PER_US = 3_690_000


def dot(left, right, left_dim, right_dim, precision=None):
    return lax.dot_general(
        left,
        right,
        (((left_dim,), (right_dim,)), ((), ())),
        precision=precision,
        preferred_element_type=F32,
    )


def col_sum(value):
    return jnp.sum(value, axis=0, keepdims=True)


def sigmoid(value):
    return 0.5 * jnp.tanh(0.5 * value) + 0.5


def per_head(rows, first, count, width):
    return jnp.concatenate(
        [jnp.broadcast_to(rows[k : k + 1], (width, rows.shape[1])) for k in range(first, first + count)]
    )


def iotas():
    down = lax.broadcasted_iota(jnp.int32, (CHUNK, CHUNK), 0)
    across = lax.broadcasted_iota(jnp.int32, (CHUNK, CHUNK), 1)
    return down, across


def step_sizes(raw, bias, log_rate):
    shifted = raw + bias
    step = jnp.maximum(shifted, 0.0) + jnp.log1p(jnp.exp(-jnp.abs(shifted)))
    rate = -jnp.exp(log_rate)
    down, across = iotas()
    upto = (down <= across).astype(F32)
    running = dot(step * (rate * LOG2E), upto, 1, 0, HIGH)
    return shifted, step, rate, running


def pair_mask(info):
    down, across = iotas()
    tags = info[0:8]
    column = jnp.transpose(tags)[:, 0:1]
    reaches = (column == info[0:1]) & (down <= across)
    return jnp.where(reaches, 0.0, FAR)


def chunk_factors(running, info):
    total = running[:, CHUNK - 1 : CHUNK]
    reach = jnp.exp2(running) * info[7:8]
    toend = jnp.exp2(total - running) * info[8:9]
    whole = jnp.exp2(jnp.broadcast_to(total, running.shape)) * info[9:10]
    return reach, toend, whole


def column_of(rows_ref, at):
    block = jnp.concatenate([rows_ref[:, at : at + CHUNK], jnp.zeros((CHUNK - 8, CHUNK), F32)])
    return jnp.transpose(block)


def shape_of(heads, inner, state):
    width = inner // heads
    return width, CHUNK // width, inner // CHUNK


def conv_block(cur, prev, taps, bias, info):
    lane = lax.broadcasted_iota(jnp.int32, cur.shape, 1)
    total = bias + taps[CONV - 1] * cur
    for k in range(1, CONV):
        mixed = jnp.where(lane >= CHUNK - k, prev, cur)
        total = total + taps[CONV - 1 - k] * (pltpu.roll(mixed, k, 1) * info[k : k + 1])
    return total


def scan_kernel(
    heads,
    inner,
    qd_ref,
    halo_ref,
    taps_ref,
    bias_ref,
    log_ref,
    skip_ref,
    info_ref,
    xa_ref,
    slope_ref,
    part_ref,
    enter_ref,
    prefix_ref,
    reach_ref,
    pack_ref,
    carry,
    wide,
    state,
    prefix,
):
    step_at = pl.program_id(0)
    last = pl.num_programs(0) - 1
    channels = xa_ref.shape[0]
    padded = bias_ref.shape[0]
    n_state = (channels - inner) // 2
    width, group, blocks = shape_of(heads, inner, n_state)

    @pl.when(step_at == 0)
    def _():
        for at in range(0, channels, CHUNK):
            columns = column_of(taps_ref, at)
            rows = halo_ref[:, at : at + CHUNK].astype(F32)
            rows = jnp.concatenate([jnp.zeros((CHUNK - EDGE, CHUNK), F32), rows])
            carry[at : at + CHUNK, :] = jnp.transpose(rows).astype(BF)
            for k in range(CONV + 1):
                wide[k, at : at + CHUNK, :] = jnp.broadcast_to(columns[:, k : k + 1], (CHUNK, CHUNK))
        state[...] = jnp.zeros_like(state)
        prefix[...] = jnp.ones_like(prefix)

    info = info_ref[...]
    raw = qd_ref[channels : channels + padded, :].astype(F32)
    _, step, _, running = step_sizes(raw, bias_ref[...], log_ref[...])
    reach, toend, whole = chunk_factors(running, info)
    before = prefix[...]
    prefix_ref[0] = before
    reach_ref[...] = before * reach
    prefix[...] = before * whole
    column = jnp.transpose(running)
    mask = pair_mask(info)
    skip = skip_ref[...]

    def active(at):
        rows = pl.ds(at, CHUNK)
        pre = conv_block(
            qd_ref[rows, :].astype(F32),
            carry[rows, :].astype(F32),
            [wide[k, rows, :] for k in range(CONV)],
            wide[CONV, rows, :],
            info,
        )
        gate = sigmoid(pre)
        value = (pre * gate).astype(BF)
        xa_ref[rows, :] = value
        slope_ref[rows, :] = (gate * (1.0 + pre * (1.0 - gate))).astype(BF)
        return value

    in_t = active(inner)
    out_t = active(inner + n_state)
    scores = dot(in_t, out_t, 0, 0)
    for block in range(blocks):
        at = block * CHUNK
        rows = pl.ds(at, CHUNK)
        x = active(at).astype(F32)
        first = block * group
        entering = state[rows, :]
        entering_low = entering.astype(BF)
        enter_ref[0, rows, :] = entering_low
        driven = x * per_head(step, first, group, width)
        total = x * per_head(skip, first, group, width) + per_head(
            reach, first, group, width
        ) * dot(entering_low, out_t, 1, 0)
        driven_low = driven.astype(BF)
        inside = []
        for k in range(group):
            head = first + k
            gap = (running[head : head + 1] + mask) - column[:, head : head + 1]
            mixer = (scores * jnp.exp2(gap)).astype(BF)
            inside.append(dot(driven_low[k * width : (k + 1) * width], mixer, 1, 0))
        part_ref[rows, :] = (total + jnp.concatenate(inside)).astype(BF)
        weighted = (driven * per_head(toend, first, group, width)).astype(BF)
        state[rows, :] = entering * per_head(whole, first, group, width) + dot(weighted, in_t, 1, 1)
    carry[...] = qd_ref[0:channels, :]

    @pl.when(step_at == last)
    def _():
        pack_ref[0:inner, :] = state[...].astype(BF)
        factor = prefix[...]
        high = factor.astype(BF)
        pack_ref[inner : inner + padded, :] = high
        pack_ref[inner + padded : inner + 2 * padded, :] = (factor - high.astype(F32)).astype(BF)


def takes(microseconds):
    return pl.CostEstimate(
        flops=0, transcendentals=0, bytes_accessed=int(microseconds * HBM_BYTES_PER_US)
    )


def lane_block(rows, lanes=CHUNK):
    return pl.BlockSpec((rows, lanes), lambda i: (0, i))


def whole_block(shape):
    return pl.BlockSpec(shape, lambda i: (0,) * len(shape))


def scan(qd, halo, taps, bias, log_rate, skip, info, heads, inner):
    length = qd.shape[1]
    padded = bias.shape[0]
    channels = qd.shape[0] - padded
    steps = length // CHUNK
    return pl.pallas_call(
        functools.partial(scan_kernel, heads, inner),
        grid=(steps,),
        in_specs=[
            lane_block(qd.shape[0]),
            whole_block(halo.shape),
            whole_block(taps.shape),
            whole_block(bias.shape),
            whole_block(bias.shape),
            whole_block(bias.shape),
            lane_block(info.shape[0]),
        ],
        out_specs=[
            lane_block(channels),
            lane_block(channels),
            lane_block(inner),
            pl.BlockSpec((1, inner, CHUNK), lambda i: (i, 0, 0)),
            pl.BlockSpec((1, padded, CHUNK), lambda i: (i, 0, 0)),
            lane_block(padded),
            whole_block((inner + 2 * padded, CHUNK)),
        ],
        out_shape=[
            jax.ShapeDtypeStruct((channels, length), BF),
            jax.ShapeDtypeStruct((channels, length), BF),
            jax.ShapeDtypeStruct((inner, length), BF),
            jax.ShapeDtypeStruct((steps, inner, CHUNK), BF),
            jax.ShapeDtypeStruct((steps, padded, CHUNK), F32),
            jax.ShapeDtypeStruct((padded, length), F32),
            jax.ShapeDtypeStruct((inner + 2 * padded, CHUNK), BF),
        ],
        scratch_shapes=[
            pltpu.VMEM((channels, CHUNK), BF),
            pltpu.VMEM((CONV + 1, channels, CHUNK), F32),
            pltpu.VMEM((inner, CHUNK), F32),
            pltpu.VMEM((padded, CHUNK), F32),
        ],
        compiler_params=pltpu.CompilerParams(vmem_limit_bytes=VMEM),
        cost_estimate=takes(20),
        name="scan_forward",
    )(qd, halo, taps, bias, log_rate, skip, info)


def joined(packs, at, inner, heads, padded):
    width = inner // heads
    first = at // width
    count = CHUNK // width
    total = None
    for pack in reversed(packs):
        own = pack[at : at + CHUNK, :].astype(F32)
        if total is not None:
            high = pack[inner : inner + padded, :].astype(F32)
            low = pack[inner + padded : inner + 2 * padded, :].astype(F32)
            own = own + per_head(high + low, first, count, width) * total
        total = own
    return total


def norm_kernel(heads, n_packs, *refs):
    packs = refs[:n_packs]
    part_ref, z_ref, out_ref, reach_ref, gain_ref, yb_ref, n_ref, enter_ref, value, gain = refs[n_packs:]
    inner = part_ref.shape[0]
    padded = reach_ref.shape[0]
    width = inner // heads
    count = CHUNK // width

    @pl.when(pl.program_id(0) == 0)
    def _():
        for at in range(0, inner, CHUNK):
            gain[at : at + CHUNK, :] = column_of(gain_ref, at)[:, 0:1]
            if n_packs:
                enter_ref[at : at + CHUNK, :] = joined(packs, at, inner, heads, padded).astype(BF)
            else:
                enter_ref[at : at + CHUNK, :] = jnp.zeros((CHUNK, CHUNK), BF)

    reach = reach_ref[...]
    value[...] = dot(enter_ref[...], out_ref[...], 1, 0)
    squares = jnp.zeros((CHUNK, reach.shape[1]), F32)
    for at in range(0, inner, CHUNK):
        rows = pl.ds(at, CHUNK)
        late = per_head(reach, at // width, count, width) * value[rows, :]
        mixed = (part_ref[rows, :].astype(F32) + late).astype(BF)
        yb_ref[rows, :] = mixed
        z = z_ref[rows, :].astype(F32)
        gated = mixed.astype(F32) * (z * sigmoid(z))
        value[rows, :] = gated
        squares = squares + gated * gated
    scale = lax.rsqrt(col_sum(squares) * (1.0 / inner) + EPS)
    for at in range(0, inner, CHUNK):
        rows = pl.ds(at, CHUNK)
        n_ref[rows, :] = (value[rows, :] * scale * gain[rows, :]).astype(BF)


def gated_norm(packs, part, z, xa, reach, gain, heads):
    inner, length = part.shape
    lanes = math.gcd(length, STEP)
    channels = xa.shape[0]
    n_state = (channels - inner) // 2
    out_at = (channels - n_state) // n_state
    return pl.pallas_call(
        functools.partial(norm_kernel, heads, len(packs)),
        grid=(length // lanes,),
        in_specs=[whole_block(pack.shape) for pack in packs]
        + [
            lane_block(inner, lanes),
            lane_block(inner, lanes),
            pl.BlockSpec((n_state, lanes), lambda i: (out_at, i)),
            lane_block(reach.shape[0], lanes),
            whole_block(gain.shape),
        ],
        out_specs=[lane_block(inner, lanes), lane_block(inner, lanes), whole_block((inner, n_state))],
        out_shape=[
            jax.ShapeDtypeStruct((inner, length), BF),
            jax.ShapeDtypeStruct((inner, length), BF),
            jax.ShapeDtypeStruct((inner, n_state), BF),
        ],
        scratch_shapes=[pltpu.VMEM((inner, lanes), F32), pltpu.VMEM((inner, 1), F32)],
        compiler_params=pltpu.CompilerParams(vmem_limit_bytes=VMEM),
        cost_estimate=takes(9),
        name="gated_norm_forward",
    )(*packs, part, z, xa, reach, gain)


def norm_back_kernel(heads, n_after, *refs):
    norm_back_step(heads, *refs[n_after:])


def norm_back_step(
    heads,
    go_ref,
    weight_ref,
    yb_ref,
    z_ref,
    out_ref,
    reach_ref,
    gain_ref,
    pack_in_ref,
    dy_ref,
    dz_ref,
    dgain_ref,
    pack_ref,
    value,
    dn,
    dgain,
    adjoint,
    far,
    gain,
):
    step_at = pl.program_id(0)
    last = pl.num_programs(0) - 1
    inner = yb_ref.shape[0]
    padded = reach_ref.shape[0]
    width = inner // heads
    count = CHUNK // width

    @pl.when(step_at == 0)
    def _():
        for at in range(0, inner, CHUNK):
            gain[at : at + CHUNK, :] = column_of(gain_ref, at)[:, 0:1]
        dgain[...] = jnp.zeros_like(dgain)
        adjoint[...] = jnp.zeros_like(adjoint)

    go = go_ref[...]
    dn[...] = dot(weight_ref[...], go, 1, 0)
    squares = jnp.zeros((CHUNK, go.shape[1]), F32)
    crosses = jnp.zeros((CHUNK, go.shape[1]), F32)
    for at in range(0, inner, CHUNK):
        rows = pl.ds(at, CHUNK)
        d_norm = dn[rows, :]
        z = z_ref[rows, :].astype(F32)
        gated = yb_ref[rows, :].astype(F32) * (z * sigmoid(z))
        value[rows, :] = gated
        squares = squares + gated * gated
        crosses = crosses + gated * (d_norm * gain[rows, :])
    scale = lax.rsqrt(col_sum(squares) * (1.0 / inner) + EPS)
    pull = col_sum(crosses) * (1.0 / inner) * scale * scale * scale
    reach = reach_ref[...]
    for at in range(0, inner, CHUNK):
        rows = pl.ds(at, CHUNK)
        gated = value[rows, :]
        d_norm = dn[rows, :]
        dgain[rows, :] += d_norm * gated * scale
        d_gated = d_norm * gain[rows, :] * scale - gated * pull
        z = z_ref[rows, :].astype(F32)
        gate = sigmoid(z)
        dy = (d_gated * (z * gate)).astype(BF)
        dy_ref[rows, :] = dy
        d_silu = d_gated * yb_ref[rows, :].astype(F32)
        dz_ref[rows, :] = (d_silu * (gate * (1.0 + z * (1.0 - gate)))).astype(BF)
        far[rows, :] = (dy.astype(F32) * per_head(reach, at // width, count, width)).astype(BF)
    adjoint[...] += dot(far[...], out_ref[...], 1, 1)

    @pl.when(step_at == last)
    def _():
        pack_ref[0:inner, :] = adjoint[...].astype(BF)
        pack_ref[inner : inner + 2 * padded, :] = pack_in_ref[inner : inner + 2 * padded, :]
        for at in range(0, inner, CHUNK):
            total = jnp.sum(dgain[at : at + CHUNK, :], axis=1, keepdims=True)
            total = jnp.transpose(jnp.broadcast_to(total, (CHUNK, CHUNK)))
            dgain_ref[:, at : at + CHUNK] = total[0:8]


def gated_norm_back(go, weight, yb, z, xa, reach, gain, pack, heads, after):
    inner, length = yb.shape
    lanes = math.gcd(length, STEP)
    channels = xa.shape[0]
    n_state = (channels - inner) // 2
    out_at = (channels - n_state) // n_state
    return pl.pallas_call(
        functools.partial(norm_back_kernel, heads, len(after)),
        grid=(length // lanes,),
        in_specs=[pl.BlockSpec(memory_space=pl.ANY)] * len(after)
        + [
            lane_block(go.shape[0], lanes),
            whole_block(weight.shape),
            lane_block(inner, lanes),
            lane_block(inner, lanes),
            pl.BlockSpec((n_state, lanes), lambda i: (out_at, i)),
            lane_block(reach.shape[0], lanes),
            whole_block(gain.shape),
            whole_block(pack.shape),
        ],
        out_specs=[
            lane_block(inner, lanes),
            lane_block(inner, lanes),
            whole_block((8, inner)),
            whole_block(pack.shape),
        ],
        out_shape=[
            jax.ShapeDtypeStruct((inner, length), BF),
            jax.ShapeDtypeStruct((inner, length), BF),
            jax.ShapeDtypeStruct((8, inner), F32),
            jax.ShapeDtypeStruct(pack.shape, BF),
        ],
        scratch_shapes=[
            pltpu.VMEM((inner, lanes), F32),
            pltpu.VMEM((inner, lanes), F32),
            pltpu.VMEM((inner, lanes), F32),
            pltpu.VMEM((inner, n_state), F32),
            pltpu.VMEM((inner, lanes), BF),
            pltpu.VMEM((inner, 1), F32),
        ],
        compiler_params=pltpu.CompilerParams(vmem_limit_bytes=VMEM),
        cost_estimate=takes(17),
        name="gated_norm_backward",
    )(*after, go, weight, yb, z, xa, reach, gain, pack)


def scan_back_kernel(heads, n_packs, n_after, *refs):
    packs = refs[:n_packs]
    (
        xa_ref,
        slope_ref,
        qd_ref,
        dy_ref,
        enter_ref,
        device_ref,
        prefix_ref,
        taps_ref,
        bias_ref,
        log_ref,
        skip_ref,
        info_ref,
        dqd_ref,
        dconv_ref,
        dhead_ref,
        edge_ref,
        wide,
        adjoint,
        later,
        dtaps,
        dhead,
        far_s,
        far_dy,
        far_g,
        far_x,
        rows_total,
        rows_leave,
        rows_direct,
        rows_skip,
        rows_pass,
        d_scores,
    ) = refs[n_packs + n_after :]
    step_at = pl.program_id(0)
    last = pl.num_programs(0) - 1
    channels = xa_ref.shape[0]
    inner = dy_ref.shape[0]
    padded = bias_ref.shape[0]
    n_state = (channels - inner) // 2
    width, group, blocks = shape_of(heads, inner, n_state)

    @pl.when(step_at == 0)
    def _():
        for at in range(0, channels, CHUNK):
            columns = column_of(taps_ref, at)
            for k in range(CONV):
                wide[k, at : at + CHUNK, :] = jnp.broadcast_to(columns[:, k : k + 1], (CHUNK, CHUNK))
        for at in range(0, inner, CHUNK):
            if n_packs:
                adjoint[at : at + CHUNK, :] = joined(packs, at, inner, heads, padded)
            else:
                adjoint[at : at + CHUNK, :] = jnp.zeros((CHUNK, CHUNK), F32)
        later[...] = jnp.zeros_like(later)
        dtaps[...] = jnp.zeros_like(dtaps)
        dhead[...] = jnp.zeros_like(dhead)
        for ref in (rows_total, rows_leave, rows_direct, rows_skip, rows_pass):
            ref[...] = jnp.zeros_like(ref)

    info = info_ref[...]
    raw = qd_ref[channels : channels + padded, :].astype(F32)
    shifted, step, rate, running = step_sizes(raw, bias_ref[...], log_ref[...])
    reach, toend, whole = chunk_factors(running, info)
    column = jnp.transpose(running)
    mask = pair_mask(info)
    skip = skip_ref[...]
    before = prefix_ref[0]
    in_t = xa_ref[inner : inner + n_state, :]
    out_t = xa_ref[inner + n_state :, :]
    scores = dot(in_t, out_t, 0, 0)
    lane = lax.broadcasted_iota(jnp.int32, (CHUNK, CHUNK), 1)

    def conv_back(at, d_active):
        rows = pl.ds(at, CHUNK)
        d_pre = d_active.astype(BF).astype(F32) * slope_ref[rows, :].astype(F32)
        q = qd_ref[rows, :].astype(F32)
        after = later[rows, :]
        dtaps[CONV, rows, :] += d_pre
        dtaps[CONV - 1, rows, :] += d_pre * q
        d_q = wide[CONV - 1, rows, :] * d_pre
        for k in range(1, CONV):
            mixed = jnp.where(lane < k, after, d_pre)
            moved = pltpu.roll(mixed, CHUNK - k, 1) * info[3 + k : 4 + k]
            d_q = d_q + wide[CONV - 1 - k, rows, :] * moved
            dtaps[CONV - 1 - k, rows, :] += moved * q
        later[rows, :] = d_pre
        dqd_ref[rows, :] = d_q.astype(BF)

    d_scores[...] = jnp.zeros_like(d_scores)
    for block in range(blocks):
        at = block * CHUNK
        rows = pl.ds(at, CHUNK)
        first = block * group
        x = xa_ref[rows, :].astype(F32)
        dy_low = dy_ref[rows, :]
        dy = dy_low.astype(F32)
        step_rows = per_head(step, first, group, width)
        entering = enter_ref[0, rows, :].astype(F32) + per_head(
            before, first, group, width
        ) * device_ref[rows, :].astype(F32)
        entering_low = entering.astype(BF)
        leaving = adjoint[rows, :]
        leaving_low = leaving.astype(BF)
        passed = entering * leaving
        driven_low = (x * step_rows).astype(BF)
        driven = driven_low.astype(F32)
        reach_dy = dy * per_head(reach, first, group, width)
        end_driven = driven * per_head(toend, first, group, width)
        far_dy_low = reach_dy.astype(BF)
        far_s[rows, :] = entering_low
        far_dy[rows, :] = far_dy_low
        far_g[rows, :] = leaving_low
        far_x[rows, :] = end_driven.astype(BF)
        far_out = reach_dy * dot(entering_low, out_t, 1, 0)
        far_in = dot(leaving_low, in_t, 1, 0)
        adjoint[rows, :] = leaving * per_head(whole, first, group, width) + dot(
            far_dy_low, out_t, 1, 1
        )
        near = []
        inside = []
        for k in range(group):
            head = first + k
            part = slice(k * width, (k + 1) * width)
            gap = (running[head : head + 1] + mask) - column[:, head : head + 1]
            decay = jnp.exp2(gap)
            mixer = (scores * decay).astype(BF)
            inside.append(dot(driven_low[part], mixer, 1, 0))
            near.append(dot(dy_low[part], mixer, 1, 1))
            d_scores[...] += decay * dot(driven_low[part], dy_low[part], 0, 0)
        near = jnp.concatenate(near)
        totals = dy * jnp.concatenate(inside) - driven * near + far_out
        leaves = end_driven * far_in
        d_driven = near + per_head(toend, first, group, width) * far_in
        direct = x * d_driven
        skips = x * dy
        for k in range(group):
            head = slice(first + k, first + k + 1)
            part = slice(k * width, (k + 1) * width)
            rows_total[head, :] = col_sum(totals[part])
            rows_leave[head, :] = col_sum(leaves[part])
            rows_direct[head, :] = col_sum(direct[part])
            rows_skip[head, :] = col_sum(skips[part])
            rows_pass[head, :] = col_sum(passed[part])
        conv_back(at, step_rows * d_driven + per_head(skip, first, group, width) * dy)
    d_scores_low = d_scores[...].astype(BF)
    d_in = dot(out_t, d_scores_low, 1, 1) + dot(far_g[...], far_x[...], 0, 0)
    d_out = dot(in_t, d_scores_low, 1, 0) + dot(far_s[...], far_dy[...], 0, 0)
    conv_back(inner, d_in)
    conv_back(inner + n_state, d_out)
    down, across = iotas()
    at_or_after = (down >= across).astype(F32)
    ahead = (down < across).astype(F32)
    through = jnp.sum(rows_pass[...], axis=1, keepdims=True) * whole
    d_rate = (
        dot(rows_total[...], at_or_after, 1, 0, HIGH)
        + dot(rows_leave[...], ahead, 1, 0, HIGH)
        + through
    )
    d_step = rows_direct[...] + rate * d_rate
    d_raw = d_step * sigmoid(shifted)
    dqd_ref[channels : channels + padded, :] = d_raw.astype(BF)
    dhead[0] += d_raw
    dhead[1] += d_rate * step * rate
    dhead[2] += rows_skip[...]

    @pl.when(step_at == last)
    def _():
        for k in range(3):
            dhead_ref[:, k : k + 1] = jnp.sum(dhead[k], axis=1, keepdims=True)
        for at in range(0, channels, CHUNK):
            totals = jnp.zeros((CHUNK, CHUNK), F32)
            for k in range(CONV + 1):
                one = jnp.sum(dtaps[k, at : at + CHUNK, :], axis=1, keepdims=True)
                totals = jnp.where(lane == k, one, totals)
            dconv_ref[:, at : at + CHUNK] = jnp.transpose(totals)[0:8]
            edge_ref[:, at : at + CHUNK] = jnp.transpose(later[at : at + CHUNK, :])[0:8, :]


def scan_back(packs, xa, slope, qd, dy, enter, device, prefix, taps, bias, log_rate, skip, info, heads, after):
    inner, length = dy.shape
    channels = xa.shape[0]
    padded = bias.shape[0]
    steps = length // CHUNK

    def back(rows):
        return pl.BlockSpec((rows, CHUNK), lambda i: (0, steps - 1 - i))

    def back_three(rows):
        return pl.BlockSpec((1, rows, CHUNK), lambda i: (steps - 1 - i, 0, 0))

    return pl.pallas_call(
        functools.partial(scan_back_kernel, heads, len(packs), len(after)),
        grid=(steps,),
        in_specs=[whole_block(pack.shape) for pack in packs]
        + [pl.BlockSpec(memory_space=pl.ANY)] * len(after)
        + [
            back(channels),
            back(channels),
            back(channels + padded),
            back(inner),
            back_three(inner),
            whole_block(device.shape),
            back_three(padded),
            whole_block(taps.shape),
            whole_block(bias.shape),
            whole_block(bias.shape),
            whole_block(bias.shape),
            back(info.shape[0]),
        ],
        out_specs=[
            back(channels + padded),
            whole_block((8, channels)),
            whole_block((padded, 8)),
            whole_block((8, channels)),
        ],
        out_shape=[
            jax.ShapeDtypeStruct((channels + padded, length), BF),
            jax.ShapeDtypeStruct((8, channels), F32),
            jax.ShapeDtypeStruct((padded, 8), F32),
            jax.ShapeDtypeStruct((8, channels), F32),
        ],
        scratch_shapes=[
            pltpu.VMEM((CONV, channels, CHUNK), F32),
            pltpu.VMEM((inner, CHUNK), F32),
            pltpu.VMEM((channels, CHUNK), F32),
            pltpu.VMEM((CONV + 1, channels, CHUNK), F32),
            pltpu.VMEM((3, padded, CHUNK), F32),
            pltpu.VMEM((inner, CHUNK), BF),
            pltpu.VMEM((inner, CHUNK), BF),
            pltpu.VMEM((inner, CHUNK), BF),
            pltpu.VMEM((inner, CHUNK), BF),
        ]
        + [pltpu.VMEM((padded, CHUNK), F32)] * 5
        + [pltpu.VMEM((CHUNK, CHUNK), F32)],
        compiler_params=pltpu.CompilerParams(vmem_limit_bytes=VMEM),
        cost_estimate=takes(33),
        name="scan_backward",
    )(*packs, *after, xa, slope, qd, dy, enter, device, prefix, taps, bias, log_rate, skip, info)


def input_back_kernel(
    token_major,
    w_ref,
    dqd_ref,
    part_ref,
    h_ref,
    gain_ref,
    grad_ref,
    out_ref,
    *refs,
):
    go_refs, (dgain_ref, d_norm, dgain, gain) = refs[:-4], refs[-4:]
    step_at = pl.program_id(0)
    last = pl.num_programs(0) - 1
    depth, lanes = h_ref.shape

    @pl.when(step_at == 0)
    def _():
        for at in range(0, depth, CHUNK):
            gain[at : at + CHUNK, :] = column_of(gain_ref, at)[:, 0:1]
        dgain[...] = jnp.zeros_like(dgain)

    d_norm[...] = dot(w_ref[...], dqd_ref[...], 1, 0) + part_ref[...]
    squares = jnp.zeros((CHUNK, lanes), F32)
    crosses = jnp.zeros((CHUNK, lanes), F32)
    for at in range(0, depth, CHUNK):
        rows = pl.ds(at, CHUNK)
        h = h_ref[rows, :]
        squares = squares + h * h
        crosses = crosses + d_norm[rows, :] * gain[rows, :] * h
    inverse = lax.rsqrt(col_sum(squares) * (1.0 / depth) + EPS)
    along = col_sum(crosses) * (1.0 / depth) * inverse * inverse * inverse
    for at in range(0, depth, CHUNK):
        rows = pl.ds(at, CHUNK)
        h = h_ref[rows, :]
        scaled = d_norm[rows, :] * inverse
        dgain[rows, :] += scaled * h
        grad = grad_ref[rows, :] + scaled * gain[rows, :] - h * along
        if token_major:
            for lane in range(0, lanes, CHUNK):
                out_ref[lane : lane + CHUNK, at : at + CHUNK] = jnp.transpose(
                    grad[:, lane : lane + CHUNK]
                )
        else:
            out_ref[rows, :] = grad
            go_refs[0][rows, :] = grad.astype(BF)

    @pl.when(step_at == last)
    def _():
        for at in range(0, depth, CHUNK):
            total = jnp.sum(dgain[at : at + CHUNK, :], axis=1, keepdims=True)
            total = jnp.transpose(jnp.broadcast_to(total, (CHUNK, CHUNK)))
            dgain_ref[:, at : at + CHUNK] = total[0:8]


def input_back(w_scan, dqd, part, hidden, gain, grad, token_major):
    depth, length = hidden.shape
    lanes = math.gcd(length, STEP)
    out_specs = [lane_block(depth, lanes), lane_block(depth, lanes)]
    out_shape = [
        jax.ShapeDtypeStruct((depth, length), F32),
        jax.ShapeDtypeStruct((depth, length), BF),
    ]
    if token_major:
        out_specs = [pl.BlockSpec((lanes, depth), lambda i: (i, 0))]
        out_shape = [jax.ShapeDtypeStruct((length, depth), F32)]
    return pl.pallas_call(
        functools.partial(input_back_kernel, token_major),
        grid=(length // lanes,),
        in_specs=[
            whole_block(w_scan.shape),
            lane_block(dqd.shape[0], lanes),
            lane_block(depth, lanes),
            lane_block(depth, lanes),
            whole_block(gain.shape),
            lane_block(depth, lanes),
        ],
        out_specs=out_specs + [whole_block((8, depth))],
        out_shape=out_shape + [jax.ShapeDtypeStruct((8, depth), F32)],
        scratch_shapes=[
            pltpu.VMEM((depth, lanes), F32),
            pltpu.VMEM((depth, lanes), F32),
            pltpu.VMEM((depth, 1), F32),
        ],
        compiler_params=pltpu.CompilerParams(vmem_limit_bytes=VMEM),
        name="input_backward",
    )(w_scan, dqd, part, hidden, gain, grad)


def edge_kernel(n_after, dqd_ref, fix_ref, *refs):
    out_ref = refs[n_after]
    channels = fix_ref.shape[1]
    out_ref[...] = dqd_ref[...]
    for at in range(0, channels, CHUNK):
        rows = pl.ds(at, CHUNK)
        fix = jnp.concatenate(
            [jnp.zeros((CHUNK - 8, CHUNK), F32), fix_ref[:, at : at + CHUNK]]
        )
        out_ref[rows, :] = (dqd_ref[rows, :].astype(F32) + jnp.transpose(fix)).astype(BF)


def edge_fix(dqd, fix, after):
    end = dqd.shape[1] // CHUNK - 1
    block = pl.BlockSpec((dqd.shape[0], CHUNK), lambda i: (0, end))
    return pl.pallas_call(
        functools.partial(edge_kernel, len(after)),
        grid=(1,),
        in_specs=[block, whole_block(fix.shape)] + [pl.BlockSpec(memory_space=pl.ANY)] * len(after),
        out_specs=block,
        out_shape=jax.ShapeDtypeStruct(dqd.shape, BF),
        input_output_aliases={0: 0},
        compiler_params=pltpu.CompilerParams(vmem_limit_bytes=VMEM),
        cost_estimate=takes(2),
        name="edge_gradient",
    )(dqd, fix, *after)


def edge_terms(edge, last_q, taps, info):
    rows = edge.shape[0]
    moved = []
    for k in range(1, CONV):
        below = jnp.concatenate([jnp.zeros((rows - k, edge.shape[1]), F32), edge[:k]])
        moved.append(below * info[3 + k, -rows:][:, None])
    fix = sum(taps[CONV - 1 - k][None, :] * moved[k - 1] for k in range(1, CONV))
    d_taps = [jnp.sum(moved[k - 1] * last_q, axis=0) for k in range(CONV - 1, 0, -1)]
    return fix, jnp.stack(d_taps)


def passed_along(block, axis, distance):
    devices = range(lax.axis_size(axis))
    route = [(i - distance, i) for i in devices if i - distance in devices]
    return lax.ppermute(block, axis, route)


def total_over(value, axis):
    size = lax.axis_size(axis)
    if size & (size - 1):
        return jnp.sum(lax.all_gather(value, axis).astype(F32), axis=0)
    terms = [value] + [
        lax.ppermute(value, axis, [(i, i ^ k) for i in range(size)]) for k in range(1, size)
    ]
    terms = [term.astype(F32) for term in terms]
    while len(terms) > 1:
        terms = [terms[k] + terms[k + 1] for k in range(0, len(terms), 2)]
    return terms[0]


def split_total_over(value, axis):
    size = lax.axis_size(axis)
    if size & (size - 1) or value.shape[0] % size:
        return lax.psum(value, axis)
    me = lax.axis_index(axis)
    parts = value.reshape((size, -1) + value.shape[1:])

    def swap(item, k):
        return lax.ppermute(item, axis, [(i, i ^ k) for i in range(size)])

    total = lax.dynamic_index_in_dim(parts, me, keepdims=False).astype(F32)
    for k in range(1, size):
        total = total + swap(lax.dynamic_index_in_dim(parts, me ^ k, keepdims=False), k).astype(F32)
    total = total.astype(value.dtype)
    for k in range(size):
        item = swap(total, k) if k else total
        parts = lax.dynamic_update_index_in_dim(parts, item, me ^ k, 0)
    return parts.reshape(value.shape)


def doubled(value, axis):
    size = lax.axis_size(axis)
    if size & (size - 1):
        return jnp.sum(lax.all_gather(value, axis), axis=0)
    bit = 1
    while bit < size:
        value = value + lax.ppermute(value, axis, [(i, i ^ bit) for i in range(size)])
        bit *= 2
    return value


def token_info(stream_ids, place, rows):
    length = stream_ids.shape[0]
    margin = CHUNK
    ids = jnp.concatenate(
        [jnp.full((margin,), -1, jnp.int32), stream_ids, jnp.full((margin,), -2, jnp.int32)]
    )
    ids = lax.dynamic_slice_in_dim(ids, place * rows, rows + 2 * margin)
    own = ids[margin : margin + rows]
    lines = [own]
    lines += [(ids[margin - k : margin - k + rows] == own) for k in range(1, CONV)]
    lines += [(ids[margin + k : margin + k + rows] == own) for k in range(1, CONV)]
    by_chunk = own.reshape(-1, CHUNK)
    before = ids[margin - 1 : margin - 1 + rows].reshape(-1, CHUNK)[:, :1]
    end = by_chunk[:, -1:]
    lines += [(by_chunk == before).reshape(-1), (by_chunk == end).reshape(-1)]
    lines += [jnp.broadcast_to(before == end, by_chunk.shape).reshape(-1)]
    lines += [jnp.zeros((rows,), jnp.int32)] * (16 - len(lines))
    return jnp.stack([line.astype(F32) for line in lines])


def body(
    tokens,
    cotangent,
    seg_ids,
    norm_gain,
    in_weight,
    dt_weight,
    conv_weight,
    conv_bias,
    dt_bias,
    a_log,
    skip,
    out_gain,
    out_weight,
):
    layers, part_d, _ = in_weight.shape
    shards = lax.axis_size("shard")
    n_seq = lax.axis_size("seq")
    place = lax.axis_index("seq")
    inner = out_weight.shape[1] * shards
    channels = conv_bias.shape[1] * shards
    heads = dt_weight.shape[2]
    padded = -(-heads // 16) * 16
    rows = tokens.shape[1]
    width_d = tokens.shape[2]
    info = token_info(seg_ids[0], place, rows)

    pieces = [norm_gain, conv_weight.reshape(layers, -1), conv_bias, out_gain]
    small = lax.all_gather(jnp.concatenate(pieces, axis=1), "shard", axis=0)
    ends = [0]
    for piece in pieces:
        ends.append(ends[-1] + piece.shape[1])
    small = [small[:, :, a:b].astype(F32) for a, b in zip(ends[:-1], ends[1:])]
    gains_in = small[0].transpose(1, 0, 2).reshape(layers, -1)
    taps_all = small[1].reshape(shards, layers, CONV, -1).transpose(1, 2, 0, 3)
    taps_all = taps_all.reshape(layers, CONV, channels)
    bias_all = small[2].transpose(1, 0, 2).reshape(layers, 1, channels)
    taps_all = jnp.concatenate(
        [taps_all, bias_all, jnp.zeros((layers, 8 - CONV - 1, channels), F32)], axis=1
    )
    gains_out = small[3].transpose(1, 0, 2).reshape(layers, 1, inner)
    gains_out = jnp.broadcast_to(gains_out, (layers, 8, inner))

    head_values = lax.all_gather(jnp.stack([dt_bias, a_log, skip]), "seq", axis=2, tiled=True)
    head_values = jnp.pad(head_values, ((0, 0), (0, 0), (0, padded - heads)))
    head_values = jnp.broadcast_to(head_values[..., None], head_values.shape + (CHUNK,))

    weights = []
    for layer in range(layers):
        scan_part = jnp.concatenate(
            [
                in_weight[layer, :, inner:],
                dt_weight[layer],
                jnp.zeros((part_d, padded - heads), in_weight.dtype),
            ],
            axis=1,
        )
        weights.append(
            (
                lax.all_gather(scan_part, "shard", axis=0, tiled=True),
                lax.all_gather(in_weight[layer, :, :inner], "shard", axis=0, tiled=True),
                lax.all_gather(out_weight[layer], "shard", axis=0, tiled=True),
            )
        )

    hidden = tokens[0].T.astype(F32)
    saved = []
    for layer in range(layers):
        w_scan, w_gate, w_out = weights[layer]
        taps = taps_all[layer]
        bias, log_rate, skips = (head_values[k, layer] for k in range(3))
        gain_out = gains_out[layer]
        inverse = lax.rsqrt(jnp.mean(hidden * hidden, axis=0, keepdims=True) + EPS)
        normed = (hidden * inverse * gains_in[layer][:, None]).astype(BF)
        halo = dot(normed[:, rows - EDGE :], w_scan, 0, 0).astype(BF)
        last_q = halo[EDGE - 8 :, :channels]
        halo = passed_along(halo, "seq", 1)
        qd = dot(w_scan, normed, 0, 0).astype(BF)
        xa, slope, part, enter, prefix, reach, pack = scan(
            qd, halo, taps, bias, log_rate, skips, info, heads, inner
        )
        packs = [passed_along(pack, "seq", k) for k in range(1, n_seq)]
        z = dot(w_gate, normed, 0, 0).astype(BF)
        yb, gated, device = gated_norm(packs, part, z, xa, reach, gain_out, heads)
        saved.append((last_q, hidden, normed, qd, xa, slope, enter, prefix, reach, pack, z, yb, gated, device))
        hidden = hidden + dot(w_out, gated, 0, 0)
    activations = hidden.astype(BF).T[None]

    go = cotangent[0].T
    grad = go.astype(F32)
    results = [None] * layers
    before_norm = []
    for layer in reversed(range(layers)):
        w_scan, w_gate, w_out = weights[layer]
        taps = taps_all[layer]
        bias, log_rate, skips = (head_values[k, layer] for k in range(3))
        gain_out = gains_out[layer]
        gain_in = jnp.broadcast_to(gains_in[layer][None], (8, width_d))
        last_q, h_in, normed, qd, xa, slope, enter, prefix, reach, pack, z, yb, gated, device = saved[layer]
        dy, dz, d_gain_out, back_pack = gated_norm_back(
            go, w_out, yb, z, xa, reach, gain_out, pack, heads, before_norm
        )
        back_packs = [passed_along(back_pack, "seq", -k) for k in range(1, n_seq)]
        d_w_out = dot(gated, go, 1, 1).astype(BF)
        d_w_gate = dot(normed, dz, 1, 1).astype(BF)
        joint = jnp.concatenate(
            [d_w_out.reshape(shards, -1, width_d)]
            + [
                d_w_gate[:, at : at + width_d].reshape(shards, part_d, width_d)
                for at in range(0, inner, width_d)
            ],
            axis=1,
        )
        share_joint = lax.psum_scatter(joint, "shard", scatter_dimension=0, tiled=True)[0]
        d_normed = dot(w_gate, dz, 1, 0)
        dqd, d_conv, d_head, edge = scan_back(
            back_packs, xa, slope, qd, dy, enter, device, prefix, taps, bias, log_rate, skips, info, heads,
            [joint, d_normed],
        )
        edge = passed_along(edge, "seq", -1)
        fix, d_taps = edge_terms(edge, last_q.astype(F32), taps, info)
        dqd = edge_fix(dqd, fix, [])
        d_w_scan = dot(normed, dqd, 1, 1).astype(BF)
        dqd, d_w_scan, share_joint = lax.optimization_barrier((dqd, d_w_scan, share_joint))
        share_scan = lax.psum_scatter(d_w_scan, "shard", scatter_dimension=0, tiled=True)
        grad, *low, d_gain_in = input_back(
            w_scan, dqd, d_normed, h_in, gain_in, grad, layer == 0
        )
        if low:
            go = low[0]
        d_gain_in = d_gain_in[0]
        shares = (share_joint, total_over(share_scan, "seq"))
        before_norm = [d_w_scan]
        conv_rows = d_conv[: CONV + 1] + jnp.pad(d_taps, ((0, 2), (0, 0)))
        pieces = [d_gain_in, conv_rows.reshape(-1), d_gain_out[0], d_head[:heads, :3].T.reshape(-1)]
        results[layer] = (shares, pieces)
    joint = jnp.concatenate([shares[0] for shares, _ in results])
    joint = split_total_over(joint, "seq").astype(F32).reshape(layers, -1, width_d)
    small = jnp.concatenate([item for _, pieces in results for item in pieces])
    small = doubled(doubled(small, "shard"), "seq")
    which = lax.axis_index("shard")

    def own(vector, index, count):
        return lax.dynamic_slice_in_dim(vector, index * count, count)

    outs = [[] for _ in range(10)]
    part_i = inner // shards
    part_c = channels // shards
    at = 0
    for share_joint, ((_, share_scan), _) in zip(joint, results):
        share_gate = jnp.concatenate(
            [share_joint[k : k + part_d] for k in range(part_i, share_joint.shape[0], part_d)], axis=1
        )
        outs[0].append(own(small[at : at + width_d], which, part_d))
        at += width_d
        outs[1].append(jnp.concatenate([share_gate, share_scan[:, :channels]], axis=1))
        outs[2].append(share_scan[:, channels : channels + heads])
        taps = small[at : at + CONV * channels].reshape(CONV, channels)
        outs[3].append(lax.dynamic_slice_in_dim(taps, which * part_c, part_c, 1))
        at += CONV * channels
        outs[4].append(own(small[at : at + channels], which, part_c))
        at += channels
        outs[8].append(own(small[at : at + inner], which, part_i))
        at += inner
        for k in range(3):
            outs[5 + k].append(own(small[at : at + heads], place, heads // n_seq))
            at += heads
        outs[9].append(share_joint[:part_i])
    return (activations, grad[None]) + tuple(jnp.stack(item) for item in outs)


def solution(mesh):
    specs = (
        P(None, "shard"),
        P(None, "shard", None),
        P(None, "shard", None),
        P(None, None, "shard"),
        P(None, "shard"),
        P(None, "seq"),
        P(None, "seq"),
        P(None, "seq"),
        P(None, "shard"),
        P(None, "shard", None),
    )
    spread = P("shard", "seq", None)
    return jax.shard_map(
        body,
        mesh=mesh,
        in_specs=(spread, spread, P("shard", None)) + specs,
        out_specs=(spread, spread) + specs,
        check_vma=False,
    )
```

```python
import functools
import math

import jax
import jax.numpy as jnp
from jax import lax
from jax.experimental import pallas as pl
from jax.experimental.pallas import tpu as pltpu
from jax.sharding import PartitionSpec as P

CONV = 4
EPS = 1e-05
CHUNK = 128
STEP = 256
EDGE = 16
LOG2E = 1.4426950408889634
FAR = -1e30
BF = jnp.bfloat16
F32 = jnp.float32
HIGH = lax.Precision.HIGHEST
VMEM = 56 * 1024 * 1024
HBM_BYTES_PER_US = 3_690_000


def dot(left, right, left_dim, right_dim, precision=None):
    return lax.dot_general(
        left,
        right,
        (((left_dim,), (right_dim,)), ((), ())),
        precision=precision,
        preferred_element_type=F32,
    )


def col_sum(value):
    return jnp.sum(value, axis=0, keepdims=True)


def sigmoid(value):
    return 0.5 * jnp.tanh(0.5 * value) + 0.5


def per_head(rows, first, count, width):
    return jnp.concatenate(
        [jnp.broadcast_to(rows[k : k + 1], (width, rows.shape[1])) for k in range(first, first + count)]
    )


def iotas():
    down = lax.broadcasted_iota(jnp.int32, (CHUNK, CHUNK), 0)
    across = lax.broadcasted_iota(jnp.int32, (CHUNK, CHUNK), 1)
    return down, across


def step_sizes(raw, bias, log_rate):
    shifted = raw + bias
    step = jnp.maximum(shifted, 0.0) + jnp.log1p(jnp.exp(-jnp.abs(shifted)))
    rate = -jnp.exp(log_rate)
    down, across = iotas()
    upto = (down <= across).astype(F32)
    running = dot(step * (rate * LOG2E), upto, 1, 0, HIGH)
    return shifted, step, rate, running


def pair_mask(info):
    down, across = iotas()
    tags = info[0:8]
    column = jnp.transpose(tags)[:, 0:1]
    reaches = (column == info[0:1]) & (down <= across)
    return jnp.where(reaches, 0.0, FAR)


def chunk_factors(running, info):
    total = running[:, CHUNK - 1 : CHUNK]
    reach = jnp.exp2(running) * info[7:8]
    toend = jnp.exp2(total - running) * info[8:9]
    whole = jnp.exp2(jnp.broadcast_to(total, running.shape)) * info[9:10]
    return reach, toend, whole


def column_of(rows_ref, at):
    block = jnp.concatenate([rows_ref[:, at : at + CHUNK], jnp.zeros((CHUNK - 8, CHUNK), F32)])
    return jnp.transpose(block)


def shape_of(heads, inner, state):
    width = inner // heads
    return width, CHUNK // width, inner // CHUNK


def conv_block(cur, prev, taps, bias, info):
    lane = lax.broadcasted_iota(jnp.int32, cur.shape, 1)
    total = bias + taps[CONV - 1] * cur
    for k in range(1, CONV):
        mixed = jnp.where(lane >= CHUNK - k, prev, cur)
        total = total + taps[CONV - 1 - k] * (pltpu.roll(mixed, k, 1) * info[k : k + 1])
    return total


def scan_kernel(
    heads,
    inner,
    qd_ref,
    halo_ref,
    taps_ref,
    bias_ref,
    log_ref,
    skip_ref,
    info_ref,
    xa_ref,
    slope_ref,
    part_ref,
    enter_ref,
    prefix_ref,
    reach_ref,
    pack_ref,
    carry,
    wide,
    state,
    prefix,
):
    step_at = pl.program_id(0)
    last = pl.num_programs(0) - 1
    channels = xa_ref.shape[0]
    padded = bias_ref.shape[0]
    n_state = (channels - inner) // 2
    width, group, blocks = shape_of(heads, inner, n_state)

    @pl.when(step_at == 0)
    def _():
        for at in range(0, channels, CHUNK):
            columns = column_of(taps_ref, at)
            rows = halo_ref[:, at : at + CHUNK].astype(F32)
            rows = jnp.concatenate([jnp.zeros((CHUNK - EDGE, CHUNK), F32), rows])
            carry[at : at + CHUNK, :] = jnp.transpose(rows).astype(BF)
            for k in range(CONV + 1):
                wide[k, at : at + CHUNK, :] = jnp.broadcast_to(columns[:, k : k + 1], (CHUNK, CHUNK))
        state[...] = jnp.zeros_like(state)
        prefix[...] = jnp.ones_like(prefix)

    info = info_ref[...]
    raw = qd_ref[channels : channels + padded, :].astype(F32)
    _, step, _, running = step_sizes(raw, bias_ref[...], log_ref[...])
    reach, toend, whole = chunk_factors(running, info)
    before = prefix[...]
    prefix_ref[0] = before
    reach_ref[...] = before * reach
    prefix[...] = before * whole
    column = jnp.transpose(running)
    mask = pair_mask(info)
    skip = skip_ref[...]

    def active(at):
        rows = pl.ds(at, CHUNK)
        pre = conv_block(
            qd_ref[rows, :].astype(F32),
            carry[rows, :].astype(F32),
            [wide[k, rows, :] for k in range(CONV)],
            wide[CONV, rows, :],
            info,
        )
        gate = sigmoid(pre)
        value = (pre * gate).astype(BF)
        xa_ref[rows, :] = value
        slope_ref[rows, :] = (gate * (1.0 + pre * (1.0 - gate))).astype(BF)
        return value

    in_t = active(inner)
    out_t = active(inner + n_state)
    scores = dot(in_t, out_t, 0, 0)
    for block in range(blocks):
        at = block * CHUNK
        rows = pl.ds(at, CHUNK)
        x = active(at).astype(F32)
        first = block * group
        entering = state[rows, :]
        entering_low = entering.astype(BF)
        enter_ref[0, rows, :] = entering_low
        driven = x * per_head(step, first, group, width)
        total = x * per_head(skip, first, group, width) + per_head(
            reach, first, group, width
        ) * dot(entering_low, out_t, 1, 0)
        driven_low = driven.astype(BF)
        inside = []
        for k in range(group):
            head = first + k
            gap = (running[head : head + 1] + mask) - column[:, head : head + 1]
            mixer = (scores * jnp.exp2(gap)).astype(BF)
            inside.append(dot(driven_low[k * width : (k + 1) * width], mixer, 1, 0))
        part_ref[rows, :] = (total + jnp.concatenate(inside)).astype(BF)
        weighted = (driven * per_head(toend, first, group, width)).astype(BF)
        state[rows, :] = entering * per_head(whole, first, group, width) + dot(weighted, in_t, 1, 1)
    carry[...] = qd_ref[0:channels, :]

    @pl.when(step_at == last)
    def _():
        pack_ref[0:inner, :] = state[...].astype(BF)
        factor = prefix[...]
        high = factor.astype(BF)
        pack_ref[inner : inner + padded, :] = high
        pack_ref[inner + padded : inner + 2 * padded, :] = (factor - high.astype(F32)).astype(BF)


def takes(microseconds):
    return pl.CostEstimate(
        flops=0, transcendentals=0, bytes_accessed=int(microseconds * HBM_BYTES_PER_US)
    )


def lane_block(rows, lanes=CHUNK):
    return pl.BlockSpec((rows, lanes), lambda i: (0, i))


def whole_block(shape):
    return pl.BlockSpec(shape, lambda i: (0,) * len(shape))


def scan(qd, halo, taps, bias, log_rate, skip, info, heads, inner):
    length = qd.shape[1]
    padded = bias.shape[0]
    channels = qd.shape[0] - padded
    steps = length // CHUNK
    return pl.pallas_call(
        functools.partial(scan_kernel, heads, inner),
        grid=(steps,),
        in_specs=[
            lane_block(qd.shape[0]),
            whole_block(halo.shape),
            whole_block(taps.shape),
            whole_block(bias.shape),
            whole_block(bias.shape),
            whole_block(bias.shape),
            lane_block(info.shape[0]),
        ],
        out_specs=[
            lane_block(channels),
            lane_block(channels),
            lane_block(inner),
            pl.BlockSpec((1, inner, CHUNK), lambda i: (i, 0, 0)),
            pl.BlockSpec((1, padded, CHUNK), lambda i: (i, 0, 0)),
            lane_block(padded),
            whole_block((inner + 2 * padded, CHUNK)),
        ],
        out_shape=[
            jax.ShapeDtypeStruct((channels, length), BF),
            jax.ShapeDtypeStruct((channels, length), BF),
            jax.ShapeDtypeStruct((inner, length), BF),
            jax.ShapeDtypeStruct((steps, inner, CHUNK), BF),
            jax.ShapeDtypeStruct((steps, padded, CHUNK), F32),
            jax.ShapeDtypeStruct((padded, length), F32),
            jax.ShapeDtypeStruct((inner + 2 * padded, CHUNK), BF),
        ],
        scratch_shapes=[
            pltpu.VMEM((channels, CHUNK), BF),
            pltpu.VMEM((CONV + 1, channels, CHUNK), F32),
            pltpu.VMEM((inner, CHUNK), F32),
            pltpu.VMEM((padded, CHUNK), F32),
        ],
        compiler_params=pltpu.CompilerParams(vmem_limit_bytes=VMEM),
        cost_estimate=takes(20),
        name="scan_forward",
    )(qd, halo, taps, bias, log_rate, skip, info)


def joined(packs, at, inner, heads, padded):
    width = inner // heads
    first = at // width
    count = CHUNK // width
    total = None
    for pack in reversed(packs):
        own = pack[at : at + CHUNK, :].astype(F32)
        if total is not None:
            high = pack[inner : inner + padded, :].astype(F32)
            low = pack[inner + padded : inner + 2 * padded, :].astype(F32)
            own = own + per_head(high + low, first, count, width) * total
        total = own
    return total


def norm_kernel(heads, n_packs, *refs):
    packs = refs[:n_packs]
    part_ref, z_ref, out_ref, reach_ref, gain_ref, yb_ref, n_ref, enter_ref, value, gain = refs[n_packs:]
    inner = part_ref.shape[0]
    padded = reach_ref.shape[0]
    width = inner // heads
    count = CHUNK // width

    @pl.when(pl.program_id(0) == 0)
    def _():
        for at in range(0, inner, CHUNK):
            gain[at : at + CHUNK, :] = column_of(gain_ref, at)[:, 0:1]
            if n_packs:
                enter_ref[at : at + CHUNK, :] = joined(packs, at, inner, heads, padded).astype(BF)
            else:
                enter_ref[at : at + CHUNK, :] = jnp.zeros((CHUNK, CHUNK), BF)

    reach = reach_ref[...]
    value[...] = dot(enter_ref[...], out_ref[...], 1, 0)
    squares = jnp.zeros((CHUNK, reach.shape[1]), F32)
    for at in range(0, inner, CHUNK):
        rows = pl.ds(at, CHUNK)
        late = per_head(reach, at // width, count, width) * value[rows, :]
        mixed = (part_ref[rows, :].astype(F32) + late).astype(BF)
        yb_ref[rows, :] = mixed
        z = z_ref[rows, :].astype(F32)
        gated = mixed.astype(F32) * (z * sigmoid(z))
        value[rows, :] = gated
        squares = squares + gated * gated
    scale = lax.rsqrt(col_sum(squares) * (1.0 / inner) + EPS)
    for at in range(0, inner, CHUNK):
        rows = pl.ds(at, CHUNK)
        n_ref[rows, :] = (value[rows, :] * scale * gain[rows, :]).astype(BF)


def gated_norm(packs, part, z, xa, reach, gain, heads):
    inner, length = part.shape
    lanes = math.gcd(length, STEP)
    channels = xa.shape[0]
    n_state = (channels - inner) // 2
    out_at = (channels - n_state) // n_state
    return pl.pallas_call(
        functools.partial(norm_kernel, heads, len(packs)),
        grid=(length // lanes,),
        in_specs=[whole_block(pack.shape) for pack in packs]
        + [
            lane_block(inner, lanes),
            lane_block(inner, lanes),
            pl.BlockSpec((n_state, lanes), lambda i: (out_at, i)),
            lane_block(reach.shape[0], lanes),
            whole_block(gain.shape),
        ],
        out_specs=[lane_block(inner, lanes), lane_block(inner, lanes), whole_block((inner, n_state))],
        out_shape=[
            jax.ShapeDtypeStruct((inner, length), BF),
            jax.ShapeDtypeStruct((inner, length), BF),
            jax.ShapeDtypeStruct((inner, n_state), BF),
        ],
        scratch_shapes=[pltpu.VMEM((inner, lanes), F32), pltpu.VMEM((inner, 1), F32)],
        compiler_params=pltpu.CompilerParams(vmem_limit_bytes=VMEM),
        cost_estimate=takes(9),
        name="gated_norm_forward",
    )(*packs, part, z, xa, reach, gain)


def norm_back_kernel(heads, n_after, *refs):
    norm_back_step(heads, *refs[n_after:])


def norm_back_step(
    heads,
    go_ref,
    weight_ref,
    yb_ref,
    z_ref,
    out_ref,
    reach_ref,
    gain_ref,
    pack_in_ref,
    dy_ref,
    dz_ref,
    dgain_ref,
    pack_ref,
    value,
    dn,
    dgain,
    adjoint,
    far,
    gain,
):
    step_at = pl.program_id(0)
    last = pl.num_programs(0) - 1
    inner = yb_ref.shape[0]
    padded = reach_ref.shape[0]
    width = inner // heads
    count = CHUNK // width

    @pl.when(step_at == 0)
    def _():
        for at in range(0, inner, CHUNK):
            gain[at : at + CHUNK, :] = column_of(gain_ref, at)[:, 0:1]
        dgain[...] = jnp.zeros_like(dgain)
        adjoint[...] = jnp.zeros_like(adjoint)

    go = go_ref[...]
    dn[...] = dot(weight_ref[...], go, 1, 0)
    squares = jnp.zeros((CHUNK, go.shape[1]), F32)
    crosses = jnp.zeros((CHUNK, go.shape[1]), F32)
    for at in range(0, inner, CHUNK):
        rows = pl.ds(at, CHUNK)
        d_norm = dn[rows, :]
        z = z_ref[rows, :].astype(F32)
        gated = yb_ref[rows, :].astype(F32) * (z * sigmoid(z))
        value[rows, :] = gated
        squares = squares + gated * gated
        crosses = crosses + gated * (d_norm * gain[rows, :])
    scale = lax.rsqrt(col_sum(squares) * (1.0 / inner) + EPS)
    pull = col_sum(crosses) * (1.0 / inner) * scale * scale * scale
    reach = reach_ref[...]
    for at in range(0, inner, CHUNK):
        rows = pl.ds(at, CHUNK)
        gated = value[rows, :]
        d_norm = dn[rows, :]
        dgain[rows, :] += d_norm * gated * scale
        d_gated = d_norm * gain[rows, :] * scale - gated * pull
        z = z_ref[rows, :].astype(F32)
        gate = sigmoid(z)
        dy = (d_gated * (z * gate)).astype(BF)
        dy_ref[rows, :] = dy
        d_silu = d_gated * yb_ref[rows, :].astype(F32)
        dz_ref[rows, :] = (d_silu * (gate * (1.0 + z * (1.0 - gate)))).astype(BF)
        far[rows, :] = (dy.astype(F32) * per_head(reach, at // width, count, width)).astype(BF)
    adjoint[...] += dot(far[...], out_ref[...], 1, 1)

    @pl.when(step_at == last)
    def _():
        pack_ref[0:inner, :] = adjoint[...].astype(BF)
        pack_ref[inner : inner + 2 * padded, :] = pack_in_ref[inner : inner + 2 * padded, :]
        for at in range(0, inner, CHUNK):
            total = jnp.sum(dgain[at : at + CHUNK, :], axis=1, keepdims=True)
            total = jnp.transpose(jnp.broadcast_to(total, (CHUNK, CHUNK)))
            dgain_ref[:, at : at + CHUNK] = total[0:8]


def gated_norm_back(go, weight, yb, z, xa, reach, gain, pack, heads, after):
    inner, length = yb.shape
    lanes = math.gcd(length, STEP)
    channels = xa.shape[0]
    n_state = (channels - inner) // 2
    out_at = (channels - n_state) // n_state
    return pl.pallas_call(
        functools.partial(norm_back_kernel, heads, len(after)),
        grid=(length // lanes,),
        in_specs=[pl.BlockSpec(memory_space=pl.ANY)] * len(after)
        + [
            lane_block(go.shape[0], lanes),
            whole_block(weight.shape),
            lane_block(inner, lanes),
            lane_block(inner, lanes),
            pl.BlockSpec((n_state, lanes), lambda i: (out_at, i)),
            lane_block(reach.shape[0], lanes),
            whole_block(gain.shape),
            whole_block(pack.shape),
        ],
        out_specs=[
            lane_block(inner, lanes),
            lane_block(inner, lanes),
            whole_block((8, inner)),
            whole_block(pack.shape),
        ],
        out_shape=[
            jax.ShapeDtypeStruct((inner, length), BF),
            jax.ShapeDtypeStruct((inner, length), BF),
            jax.ShapeDtypeStruct((8, inner), F32),
            jax.ShapeDtypeStruct(pack.shape, BF),
        ],
        scratch_shapes=[
            pltpu.VMEM((inner, lanes), F32),
            pltpu.VMEM((inner, lanes), F32),
            pltpu.VMEM((inner, lanes), F32),
            pltpu.VMEM((inner, n_state), F32),
            pltpu.VMEM((inner, lanes), BF),
            pltpu.VMEM((inner, 1), F32),
        ],
        compiler_params=pltpu.CompilerParams(vmem_limit_bytes=VMEM),
        cost_estimate=takes(17),
        name="gated_norm_backward",
    )(*after, go, weight, yb, z, xa, reach, gain, pack)


def scan_back_kernel(heads, n_packs, n_after, *refs):
    packs = refs[:n_packs]
    (
        xa_ref,
        slope_ref,
        qd_ref,
        dy_ref,
        enter_ref,
        device_ref,
        prefix_ref,
        taps_ref,
        bias_ref,
        log_ref,
        skip_ref,
        info_ref,
        dqd_ref,
        dconv_ref,
        dhead_ref,
        edge_ref,
        wide,
        adjoint,
        later,
        dtaps,
        dhead,
        far_s,
        far_dy,
        far_g,
        far_x,
        rows_total,
        rows_leave,
        rows_direct,
        rows_skip,
        rows_pass,
        d_scores,
    ) = refs[n_packs + n_after :]
    step_at = pl.program_id(0)
    last = pl.num_programs(0) - 1
    channels = xa_ref.shape[0]
    inner = dy_ref.shape[0]
    padded = bias_ref.shape[0]
    n_state = (channels - inner) // 2
    width, group, blocks = shape_of(heads, inner, n_state)

    @pl.when(step_at == 0)
    def _():
        for at in range(0, channels, CHUNK):
            columns = column_of(taps_ref, at)
            for k in range(CONV):
                wide[k, at : at + CHUNK, :] = jnp.broadcast_to(columns[:, k : k + 1], (CHUNK, CHUNK))
        for at in range(0, inner, CHUNK):
            if n_packs:
                adjoint[at : at + CHUNK, :] = joined(packs, at, inner, heads, padded)
            else:
                adjoint[at : at + CHUNK, :] = jnp.zeros((CHUNK, CHUNK), F32)
        later[...] = jnp.zeros_like(later)
        dtaps[...] = jnp.zeros_like(dtaps)
        dhead[...] = jnp.zeros_like(dhead)
        for ref in (rows_total, rows_leave, rows_direct, rows_skip, rows_pass):
            ref[...] = jnp.zeros_like(ref)

    info = info_ref[...]
    raw = qd_ref[channels : channels + padded, :].astype(F32)
    shifted, step, rate, running = step_sizes(raw, bias_ref[...], log_ref[...])
    reach, toend, whole = chunk_factors(running, info)
    column = jnp.transpose(running)
    mask = pair_mask(info)
    skip = skip_ref[...]
    before = prefix_ref[0]
    in_t = xa_ref[inner : inner + n_state, :]
    out_t = xa_ref[inner + n_state :, :]
    scores = dot(in_t, out_t, 0, 0)
    lane = lax.broadcasted_iota(jnp.int32, (CHUNK, CHUNK), 1)

    def conv_back(at, d_active):
        rows = pl.ds(at, CHUNK)
        d_pre = d_active.astype(BF).astype(F32) * slope_ref[rows, :].astype(F32)
        q = qd_ref[rows, :].astype(F32)
        after = later[rows, :]
        dtaps[CONV, rows, :] += d_pre
        dtaps[CONV - 1, rows, :] += d_pre * q
        d_q = wide[CONV - 1, rows, :] * d_pre
        for k in range(1, CONV):
            mixed = jnp.where(lane < k, after, d_pre)
            moved = pltpu.roll(mixed, CHUNK - k, 1) * info[3 + k : 4 + k]
            d_q = d_q + wide[CONV - 1 - k, rows, :] * moved
            dtaps[CONV - 1 - k, rows, :] += moved * q
        later[rows, :] = d_pre
        dqd_ref[rows, :] = d_q.astype(BF)

    d_scores[...] = jnp.zeros_like(d_scores)
    for block in range(blocks):
        at = block * CHUNK
        rows = pl.ds(at, CHUNK)
        first = block * group
        x = xa_ref[rows, :].astype(F32)
        dy_low = dy_ref[rows, :]
        dy = dy_low.astype(F32)
        step_rows = per_head(step, first, group, width)
        entering = enter_ref[0, rows, :].astype(F32) + per_head(
            before, first, group, width
        ) * device_ref[rows, :].astype(F32)
        entering_low = entering.astype(BF)
        leaving = adjoint[rows, :]
        leaving_low = leaving.astype(BF)
        passed = entering * leaving
        driven_low = (x * step_rows).astype(BF)
        driven = driven_low.astype(F32)
        reach_dy = dy * per_head(reach, first, group, width)
        end_driven = driven * per_head(toend, first, group, width)
        far_dy_low = reach_dy.astype(BF)
        far_s[rows, :] = entering_low
        far_dy[rows, :] = far_dy_low
        far_g[rows, :] = leaving_low
        far_x[rows, :] = end_driven.astype(BF)
        far_out = reach_dy * dot(entering_low, out_t, 1, 0)
        far_in = dot(leaving_low, in_t, 1, 0)
        adjoint[rows, :] = leaving * per_head(whole, first, group, width) + dot(
            far_dy_low, out_t, 1, 1
        )
        near = []
        inside = []
        for k in range(group):
            head = first + k
            part = slice(k * width, (k + 1) * width)
            gap = (running[head : head + 1] + mask) - column[:, head : head + 1]
            decay = jnp.exp2(gap)
            mixer = (scores * decay).astype(BF)
            inside.append(dot(driven_low[part], mixer, 1, 0))
            near.append(dot(dy_low[part], mixer, 1, 1))
            d_scores[...] += decay * dot(driven_low[part], dy_low[part], 0, 0)
        near = jnp.concatenate(near)
        totals = dy * jnp.concatenate(inside) - driven * near + far_out
        leaves = end_driven * far_in
        d_driven = near + per_head(toend, first, group, width) * far_in
        direct = x * d_driven
        skips = x * dy
        for k in range(group):
            head = slice(first + k, first + k + 1)
            part = slice(k * width, (k + 1) * width)
            rows_total[head, :] = col_sum(totals[part])
            rows_leave[head, :] = col_sum(leaves[part])
            rows_direct[head, :] = col_sum(direct[part])
            rows_skip[head, :] = col_sum(skips[part])
            rows_pass[head, :] = col_sum(passed[part])
        conv_back(at, step_rows * d_driven + per_head(skip, first, group, width) * dy)
    d_scores_low = d_scores[...].astype(BF)
    d_in = dot(out_t, d_scores_low, 1, 1) + dot(far_g[...], far_x[...], 0, 0)
    d_out = dot(in_t, d_scores_low, 1, 0) + dot(far_s[...], far_dy[...], 0, 0)
    conv_back(inner, d_in)
    conv_back(inner + n_state, d_out)
    down, across = iotas()
    at_or_after = (down >= across).astype(F32)
    ahead = (down < across).astype(F32)
    through = jnp.sum(rows_pass[...], axis=1, keepdims=True) * whole
    d_rate = (
        dot(rows_total[...], at_or_after, 1, 0, HIGH)
        + dot(rows_leave[...], ahead, 1, 0, HIGH)
        + through
    )
    d_step = rows_direct[...] + rate * d_rate
    d_raw = d_step * sigmoid(shifted)
    dqd_ref[channels : channels + padded, :] = d_raw.astype(BF)
    dhead[0] += d_raw
    dhead[1] += d_rate * step * rate
    dhead[2] += rows_skip[...]

    @pl.when(step_at == last)
    def _():
        for k in range(3):
            dhead_ref[:, k : k + 1] = jnp.sum(dhead[k], axis=1, keepdims=True)
        for at in range(0, channels, CHUNK):
            totals = jnp.zeros((CHUNK, CHUNK), F32)
            for k in range(CONV + 1):
                one = jnp.sum(dtaps[k, at : at + CHUNK, :], axis=1, keepdims=True)
                totals = jnp.where(lane == k, one, totals)
            dconv_ref[:, at : at + CHUNK] = jnp.transpose(totals)[0:8]
            edge_ref[:, at : at + CHUNK] = jnp.transpose(later[at : at + CHUNK, :])[0:8, :]


def scan_back(packs, xa, slope, qd, dy, enter, device, prefix, taps, bias, log_rate, skip, info, heads, after):
    inner, length = dy.shape
    channels = xa.shape[0]
    padded = bias.shape[0]
    steps = length // CHUNK

    def back(rows):
        return pl.BlockSpec((rows, CHUNK), lambda i: (0, steps - 1 - i))

    def back_three(rows):
        return pl.BlockSpec((1, rows, CHUNK), lambda i: (steps - 1 - i, 0, 0))

    return pl.pallas_call(
        functools.partial(scan_back_kernel, heads, len(packs), len(after)),
        grid=(steps,),
        in_specs=[whole_block(pack.shape) for pack in packs]
        + [pl.BlockSpec(memory_space=pl.ANY)] * len(after)
        + [
            back(channels),
            back(channels),
            back(channels + padded),
            back(inner),
            back_three(inner),
            whole_block(device.shape),
            back_three(padded),
            whole_block(taps.shape),
            whole_block(bias.shape),
            whole_block(bias.shape),
            whole_block(bias.shape),
            back(info.shape[0]),
        ],
        out_specs=[
            back(channels + padded),
            whole_block((8, channels)),
            whole_block((padded, 8)),
            whole_block((8, channels)),
        ],
        out_shape=[
            jax.ShapeDtypeStruct((channels + padded, length), BF),
            jax.ShapeDtypeStruct((8, channels), F32),
            jax.ShapeDtypeStruct((padded, 8), F32),
            jax.ShapeDtypeStruct((8, channels), F32),
        ],
        scratch_shapes=[
            pltpu.VMEM((CONV, channels, CHUNK), F32),
            pltpu.VMEM((inner, CHUNK), F32),
            pltpu.VMEM((channels, CHUNK), F32),
            pltpu.VMEM((CONV + 1, channels, CHUNK), F32),
            pltpu.VMEM((3, padded, CHUNK), F32),
            pltpu.VMEM((inner, CHUNK), BF),
            pltpu.VMEM((inner, CHUNK), BF),
            pltpu.VMEM((inner, CHUNK), BF),
            pltpu.VMEM((inner, CHUNK), BF),
        ]
        + [pltpu.VMEM((padded, CHUNK), F32)] * 5
        + [pltpu.VMEM((CHUNK, CHUNK), F32)],
        compiler_params=pltpu.CompilerParams(vmem_limit_bytes=VMEM),
        cost_estimate=takes(33),
        name="scan_backward",
    )(*packs, *after, xa, slope, qd, dy, enter, device, prefix, taps, bias, log_rate, skip, info)


def input_back_kernel(
    token_major,
    w_ref,
    dqd_ref,
    part_ref,
    h_ref,
    gain_ref,
    grad_ref,
    out_ref,
    *refs,
):
    go_refs, (dgain_ref, d_norm, dgain, gain) = refs[:-4], refs[-4:]
    step_at = pl.program_id(0)
    last = pl.num_programs(0) - 1
    depth, lanes = h_ref.shape

    @pl.when(step_at == 0)
    def _():
        for at in range(0, depth, CHUNK):
            gain[at : at + CHUNK, :] = column_of(gain_ref, at)[:, 0:1]
        dgain[...] = jnp.zeros_like(dgain)

    d_norm[...] = dot(w_ref[...], dqd_ref[...], 1, 0) + part_ref[...]
    squares = jnp.zeros((CHUNK, lanes), F32)
    crosses = jnp.zeros((CHUNK, lanes), F32)
    for at in range(0, depth, CHUNK):
        rows = pl.ds(at, CHUNK)
        h = h_ref[rows, :].astype(F32)
        squares = squares + h * h
        crosses = crosses + d_norm[rows, :] * gain[rows, :] * h
    inverse = lax.rsqrt(col_sum(squares) * (1.0 / depth) + EPS)
    along = col_sum(crosses) * (1.0 / depth) * inverse * inverse * inverse
    for at in range(0, depth, CHUNK):
        rows = pl.ds(at, CHUNK)
        h = h_ref[rows, :].astype(F32)
        scaled = d_norm[rows, :] * inverse
        dgain[rows, :] += scaled * h
        grad = grad_ref[rows, :].astype(F32) + scaled * gain[rows, :] - h * along
        if token_major:
            for lane in range(0, lanes, CHUNK):
                out_ref[lane : lane + CHUNK, at : at + CHUNK] = jnp.transpose(
                    grad[:, lane : lane + CHUNK]
                )
        else:
            out_ref[rows, :] = grad
            go_refs[0][rows, :] = grad.astype(BF)

    @pl.when(step_at == last)
    def _():
        for at in range(0, depth, CHUNK):
            total = jnp.sum(dgain[at : at + CHUNK, :], axis=1, keepdims=True)
            total = jnp.transpose(jnp.broadcast_to(total, (CHUNK, CHUNK)))
            dgain_ref[:, at : at + CHUNK] = total[0:8]


def input_back(w_scan, dqd, part, hidden, gain, grad, token_major):
    depth, length = hidden.shape
    lanes = math.gcd(length, STEP)
    out_specs = [lane_block(depth, lanes), lane_block(depth, lanes)]
    out_shape = [
        jax.ShapeDtypeStruct((depth, length), F32),
        jax.ShapeDtypeStruct((depth, length), BF),
    ]
    if token_major:
        out_specs = [pl.BlockSpec((lanes, depth), lambda i: (i, 0))]
        out_shape = [jax.ShapeDtypeStruct((length, depth), F32)]
    return pl.pallas_call(
        functools.partial(input_back_kernel, token_major),
        grid=(length // lanes,),
        in_specs=[
            whole_block(w_scan.shape),
            lane_block(dqd.shape[0], lanes),
            lane_block(depth, lanes),
            lane_block(depth, lanes),
            whole_block(gain.shape),
            lane_block(depth, lanes),
        ],
        out_specs=out_specs + [whole_block((8, depth))],
        out_shape=out_shape + [jax.ShapeDtypeStruct((8, depth), F32)],
        scratch_shapes=[
            pltpu.VMEM((depth, lanes), F32),
            pltpu.VMEM((depth, lanes), F32),
            pltpu.VMEM((depth, 1), F32),
        ],
        compiler_params=pltpu.CompilerParams(vmem_limit_bytes=VMEM),
        name="input_backward",
    )(w_scan, dqd, part, hidden, gain, grad)


def edge_kernel(n_after, dqd_ref, fix_ref, *refs):
    out_ref = refs[n_after]
    channels = fix_ref.shape[1]
    out_ref[...] = dqd_ref[...]
    for at in range(0, channels, CHUNK):
        rows = pl.ds(at, CHUNK)
        fix = jnp.concatenate(
            [jnp.zeros((CHUNK - 8, CHUNK), F32), fix_ref[:, at : at + CHUNK]]
        )
        out_ref[rows, :] = (dqd_ref[rows, :].astype(F32) + jnp.transpose(fix)).astype(BF)


def edge_fix(dqd, fix, after):
    end = dqd.shape[1] // CHUNK - 1
    block = pl.BlockSpec((dqd.shape[0], CHUNK), lambda i: (0, end))
    return pl.pallas_call(
        functools.partial(edge_kernel, len(after)),
        grid=(1,),
        in_specs=[block, whole_block(fix.shape)] + [pl.BlockSpec(memory_space=pl.ANY)] * len(after),
        out_specs=block,
        out_shape=jax.ShapeDtypeStruct(dqd.shape, BF),
        input_output_aliases={0: 0},
        compiler_params=pltpu.CompilerParams(vmem_limit_bytes=VMEM),
        cost_estimate=takes(2),
        name="edge_gradient",
    )(dqd, fix, *after)


def edge_terms(edge, last_q, taps, info):
    rows = edge.shape[0]
    moved = []
    for k in range(1, CONV):
        below = jnp.concatenate([jnp.zeros((rows - k, edge.shape[1]), F32), edge[:k]])
        moved.append(below * info[3 + k, -rows:][:, None])
    fix = sum(taps[CONV - 1 - k][None, :] * moved[k - 1] for k in range(1, CONV))
    d_taps = [jnp.sum(moved[k - 1] * last_q, axis=0) for k in range(CONV - 1, 0, -1)]
    return fix, jnp.stack(d_taps)


def passed_along(block, axis, distance):
    devices = range(lax.axis_size(axis))
    route = [(i - distance, i) for i in devices if i - distance in devices]
    return lax.ppermute(block, axis, route)


def total_over(value, axis):
    size = lax.axis_size(axis)
    if size & (size - 1):
        return jnp.sum(lax.all_gather(value, axis).astype(F32), axis=0)
    terms = [value] + [
        lax.ppermute(value, axis, [(i, i ^ k) for i in range(size)]) for k in range(1, size)
    ]
    terms = [term.astype(F32) for term in terms]
    while len(terms) > 1:
        terms = [terms[k] + terms[k + 1] for k in range(0, len(terms), 2)]
    return terms[0]


def split_total_over(value, axis):
    size = lax.axis_size(axis)
    if size & (size - 1) or value.shape[0] % size:
        return lax.psum(value, axis)
    me = lax.axis_index(axis)
    parts = value.reshape((size, -1) + value.shape[1:])

    def swap(item, k):
        return lax.ppermute(item, axis, [(i, i ^ k) for i in range(size)])

    total = lax.dynamic_index_in_dim(parts, me, keepdims=False).astype(F32)
    for k in range(1, size):
        total = total + swap(lax.dynamic_index_in_dim(parts, me ^ k, keepdims=False), k).astype(F32)
    total = total.astype(value.dtype)
    for k in range(size):
        item = swap(total, k) if k else total
        parts = lax.dynamic_update_index_in_dim(parts, item, me ^ k, 0)
    return parts.reshape(value.shape)


def doubled(value, axis):
    size = lax.axis_size(axis)
    if size & (size - 1):
        return jnp.sum(lax.all_gather(value, axis), axis=0)
    bit = 1
    while bit < size:
        value = value + lax.ppermute(value, axis, [(i, i ^ bit) for i in range(size)])
        bit *= 2
    return value


def token_info(stream_ids, place, rows):
    length = stream_ids.shape[0]
    margin = CHUNK
    ids = jnp.concatenate(
        [jnp.full((margin,), -1, jnp.int32), stream_ids, jnp.full((margin,), -2, jnp.int32)]
    )
    ids = lax.dynamic_slice_in_dim(ids, place * rows, rows + 2 * margin)
    own = ids[margin : margin + rows]
    lines = [own]
    lines += [(ids[margin - k : margin - k + rows] == own) for k in range(1, CONV)]
    lines += [(ids[margin + k : margin + k + rows] == own) for k in range(1, CONV)]
    by_chunk = own.reshape(-1, CHUNK)
    before = ids[margin - 1 : margin - 1 + rows].reshape(-1, CHUNK)[:, :1]
    end = by_chunk[:, -1:]
    lines += [(by_chunk == before).reshape(-1), (by_chunk == end).reshape(-1)]
    lines += [jnp.broadcast_to(before == end, by_chunk.shape).reshape(-1)]
    lines += [jnp.zeros((rows,), jnp.int32)] * (16 - len(lines))
    return jnp.stack([line.astype(F32) for line in lines])


def body(
    tokens,
    cotangent,
    seg_ids,
    norm_gain,
    in_weight,
    dt_weight,
    conv_weight,
    conv_bias,
    dt_bias,
    a_log,
    skip,
    out_gain,
    out_weight,
):
    layers, part_d, _ = in_weight.shape
    shards = lax.axis_size("shard")
    n_seq = lax.axis_size("seq")
    place = lax.axis_index("seq")
    inner = out_weight.shape[1] * shards
    channels = conv_bias.shape[1] * shards
    heads = dt_weight.shape[2]
    padded = -(-heads // 16) * 16
    rows = tokens.shape[1]
    width_d = tokens.shape[2]
    info = token_info(seg_ids[0], place, rows)

    pieces = [norm_gain, conv_weight.reshape(layers, -1), conv_bias, out_gain]
    small = lax.all_gather(jnp.concatenate(pieces, axis=1), "shard", axis=0)
    ends = [0]
    for piece in pieces:
        ends.append(ends[-1] + piece.shape[1])
    small = [small[:, :, a:b].astype(F32) for a, b in zip(ends[:-1], ends[1:])]
    gains_in = small[0].transpose(1, 0, 2).reshape(layers, -1)
    taps_all = small[1].reshape(shards, layers, CONV, -1).transpose(1, 2, 0, 3)
    taps_all = taps_all.reshape(layers, CONV, channels)
    bias_all = small[2].transpose(1, 0, 2).reshape(layers, 1, channels)
    taps_all = jnp.concatenate(
        [taps_all, bias_all, jnp.zeros((layers, 8 - CONV - 1, channels), F32)], axis=1
    )
    gains_out = small[3].transpose(1, 0, 2).reshape(layers, 1, inner)
    gains_out = jnp.broadcast_to(gains_out, (layers, 8, inner))

    head_values = lax.all_gather(jnp.stack([dt_bias, a_log, skip]), "seq", axis=2, tiled=True)
    head_values = jnp.pad(head_values, ((0, 0), (0, 0), (0, padded - heads)))
    head_values = jnp.broadcast_to(head_values[..., None], head_values.shape + (CHUNK,))

    weights = []
    for layer in range(layers):
        scan_part = jnp.concatenate(
            [
                in_weight[layer, :, inner:],
                dt_weight[layer],
                jnp.zeros((part_d, padded - heads), in_weight.dtype),
            ],
            axis=1,
        )
        weights.append(
            (
                lax.all_gather(scan_part, "shard", axis=0, tiled=True),
                lax.all_gather(in_weight[layer, :, :inner], "shard", axis=0, tiled=True),
                lax.all_gather(out_weight[layer], "shard", axis=0, tiled=True),
            )
        )

    first = tokens[0].T
    hidden = first.astype(F32)
    saved = []
    for layer in range(layers):
        w_scan, w_gate, w_out = weights[layer]
        taps = taps_all[layer]
        bias, log_rate, skips = (head_values[k, layer] for k in range(3))
        gain_out = gains_out[layer]
        inverse = lax.rsqrt(jnp.mean(hidden * hidden, axis=0, keepdims=True) + EPS)
        normed = (hidden * inverse * gains_in[layer][:, None]).astype(BF)
        halo = dot(normed[:, rows - EDGE :], w_scan, 0, 0).astype(BF)
        last_q = halo[EDGE - 8 :, :channels]
        halo = passed_along(halo, "seq", 1)
        qd = dot(w_scan, normed, 0, 0).astype(BF)
        xa, slope, part, enter, prefix, reach, pack = scan(
            qd, halo, taps, bias, log_rate, skips, info, heads, inner
        )
        packs = [passed_along(pack, "seq", k) for k in range(1, n_seq)]
        z = dot(w_gate, normed, 0, 0).astype(BF)
        yb, gated, device = gated_norm(packs, part, z, xa, reach, gain_out, heads)
        saved.append((last_q, hidden, normed, qd, xa, slope, enter, prefix, reach, pack, z, yb, gated, device))
        hidden = hidden + dot(w_out, gated, 0, 0)
    activations = hidden.astype(BF).T[None]

    go = grad = cotangent[0].T
    results = [None] * layers
    before_norm = []
    for layer in reversed(range(layers)):
        w_scan, w_gate, w_out = weights[layer]
        taps = taps_all[layer]
        bias, log_rate, skips = (head_values[k, layer] for k in range(3))
        gain_out = gains_out[layer]
        gain_in = jnp.broadcast_to(gains_in[layer][None], (8, width_d))
        last_q, h_in, normed, qd, xa, slope, enter, prefix, reach, pack, z, yb, gated, device = saved[layer]
        dy, dz, d_gain_out, back_pack = gated_norm_back(
            go, w_out, yb, z, xa, reach, gain_out, pack, heads, before_norm
        )
        back_packs = []
        for k in reversed(range(1, n_seq)):
            if back_packs and layer == 0:
                back_pack, back_packs[0] = lax.optimization_barrier((back_pack, back_packs[0]))
            back_packs.insert(0, passed_along(back_pack, "seq", -k))
        d_w_out = dot(gated, go, 1, 1).astype(BF)
        d_w_gate = dot(normed, dz, 1, 1).astype(BF)
        joint = jnp.concatenate(
            [d_w_out.reshape(shards, -1, width_d)]
            + [
                d_w_gate[:, at : at + width_d].reshape(shards, part_d, width_d)
                for at in range(0, inner, width_d)
            ],
            axis=1,
        )
        share_joint = lax.psum_scatter(joint, "shard", scatter_dimension=0, tiled=True)[0]
        d_normed = dot(w_gate, dz, 1, 0)
        dqd, d_conv, d_head, edge = scan_back(
            back_packs, xa, slope, qd, dy, enter, device, prefix, taps, bias, log_rate, skips, info, heads,
            [joint, d_normed],
        )
        edge = passed_along(edge, "seq", -1)
        fix, d_taps = edge_terms(edge, last_q.astype(F32), taps, info)
        dqd = edge_fix(dqd, fix, [])
        d_w_scan = dot(normed, dqd, 1, 1).astype(BF)
        dqd, d_w_scan, share_joint = lax.optimization_barrier((dqd, d_w_scan, share_joint))
        share_scan = lax.psum_scatter(d_w_scan, "shard", scatter_dimension=0, tiled=True)
        grad, *low, d_gain_in = input_back(
            w_scan, dqd, d_normed, h_in if layer else first, gain_in, grad, layer == 0
        )
        if low:
            go = low[0]
        d_gain_in = d_gain_in[0]
        shares = (share_joint, total_over(share_scan, "seq"))
        before_norm = [d_w_scan]
        conv_rows = d_conv[: CONV + 1] + jnp.pad(d_taps, ((0, 2), (0, 0)))
        pieces = [d_gain_in, conv_rows.reshape(-1), d_gain_out[0], d_head[:heads, :3].T.reshape(-1)]
        results[layer] = (shares, pieces)
    joint = jnp.concatenate([shares[0] for shares, _ in results])
    joint = split_total_over(joint, "seq").astype(F32).reshape(layers, -1, width_d)
    small = jnp.concatenate([item for _, pieces in results for item in pieces])
    small = doubled(doubled(small, "shard"), "seq")
    which = lax.axis_index("shard")

    def own(vector, index, count):
        return lax.dynamic_slice_in_dim(vector, index * count, count)

    outs = [[] for _ in range(10)]
    part_i = inner // shards
    part_c = channels // shards
    at = 0
    for share_joint, ((_, share_scan), _) in zip(joint, results):
        share_gate = jnp.concatenate(
            [share_joint[k : k + part_d] for k in range(part_i, share_joint.shape[0], part_d)], axis=1
        )
        outs[0].append(own(small[at : at + width_d], which, part_d))
        at += width_d
        outs[1].append(jnp.concatenate([share_gate, share_scan[:, :channels]], axis=1))
        outs[2].append(share_scan[:, channels : channels + heads])
        taps = small[at : at + CONV * channels].reshape(CONV, channels)
        outs[3].append(lax.dynamic_slice_in_dim(taps, which * part_c, part_c, 1))
        at += CONV * channels
        outs[4].append(own(small[at : at + channels], which, part_c))
        at += channels
        outs[8].append(own(small[at : at + inner], which, part_i))
        at += inner
        for k in range(3):
            outs[5 + k].append(own(small[at : at + heads], place, heads // n_seq))
            at += heads
        outs[9].append(share_joint[:part_i])
    return (activations, grad[None]) + tuple(jnp.stack(item) for item in outs)


def solution(mesh):
    specs = (
        P(None, "shard"),
        P(None, "shard", None),
        P(None, "shard", None),
        P(None, None, "shard"),
        P(None, "shard"),
        P(None, "seq"),
        P(None, "seq"),
        P(None, "seq"),
        P(None, "shard"),
        P(None, "shard", None),
    )
    spread = P("shard", "seq", None)
    return jax.shard_map(
        body,
        mesh=mesh,
        in_specs=(spread, spread, P("shard", None)) + specs,
        out_specs=(spread, spread) + specs,
        check_vma=False,
    )
```
